32 devices in a mesh: group: 2 (over y), exp: 4 (over z), tok: 4 (over x, core).
Axes of the slice: x: 2, y: 2, z: 4, core: 2. Of those that a mesh axis runs over, the one named last changes fastest.
Arguments:
- activations: bfloat16 [1024, 2048], P(('group', 'exp'), 'tok'), parts along dimension 0, may hold values from -6 to 6
- expert_ids: int32 [1024, 4], P(('group', 'exp')), parts along dimension 0, may hold values from 0 to 7, all different within a row; in each aligned block of 128 rows (0 to 127, 128 to 255, ...) at most 128 rows name the same one
- gate_values: float32 [1024, 4], P(('group', 'exp')), parts along dimension 0, may hold values from 0.2 to 1
- expert_gate: bfloat16 [8, 2048, 512], P('exp', 'tok'), may hold values from -0.125 to 0.125
- expert_up: bfloat16 [8, 2048, 512], P('exp', 'tok'), may hold values from -0.125 to 0.125
- expert_down: bfloat16 [8, 512, 2048], P('exp', None, 'tok'), may hold values from -0.25 to 0.25
Outputs:
- layer_out: bfloat16 [1024, 2048], P(('group', 'exp'), 'tok'), parts along dimension 0
The draws below stay inside these ranges and needn't reach their ends.
There are 2 independent parts, one for each index of `group`. The reference program is written for one: setup_inputs(seed, part) draws one part's arguments, and reference() takes and returns one part's arrays. A program takes and returns all parts, laid end to end along the dimension named above; an argument that names none is the same for every part. Nothing has to cross between parts.
Inputs may be any that keep to these rules, and one draw needn't show every extreme that they name: `expert_ids`: each row names 4 different experts. Within each aligned block of 128 rows (the tokens of one index of exp) no expert is named by more than 128 rows, and in every draw some expert is named by exactly 128 rows of some block.
All inputs are finite; a program needn't handle non-finite values.
Results may differ from the reference program's by a relative error of at most 0.023.
Values may be sent and summed in bfloat16 or wider, within the bound.
No kernel may reach another device: no remote copies, remote signals or barrier semaphores. Data moves between devices by JAX's collectives and lax.ppermute only.
A program may use at most 64 MiB of HBM per device.

```python
import math
import jax
import jax.numpy as jnp
import numpy as np
from jax import lax

D = 2048
FF = 512
TOP = 4
TOK_DEV = 128
EXPERTS = 8
CAP = 128
TOKENS = 512
N_EXP = 4
N_TOK = 4


def block_levels(stream_key, shape, shards, low, largest):
    gain, own = 1.0, jax.random.fold_in(stream_key, 6)
    for position, blocks in shards:
        steps = jnp.exp(jax.random.uniform(jax.random.fold_in(own, position), (blocks,), jnp.float32, low / len(shards), largest / len(shards)))
        gain = gain * jnp.repeat(steps, shape[position] // blocks).reshape([-1 if axis == position else 1 for axis in range(len(shape))])
    return gain


def assign_block(own_key, own, number, rows, amount, top, most, skew):
    sequence = jax.random.permutation(own_key, amount)
    heavy_load, usual = load_shares(amount, rows * top, most, skew, True), load_shares(amount, rows * top, most, skew, False)
    places = jnp.arange(amount)

    def named(sizes, offset_by):
        used = int((sizes > 0).sum())
        fixed = max(1, used // 4)
        shifted = fixed + (places - fixed + offset_by * (used - fixed)) % max(1, amount - fixed)
        return jnp.zeros((amount,), jnp.int32).at[sequence[jnp.where(places < fixed, places, shifted)]].set(jnp.asarray(sizes, jnp.int32))

    sizes = jnp.where(number % 4 == 0, named(heavy_load, number // 4), named(usual, number - number // 4 - 1))
    mixed = jax.random.permutation(jax.random.fold_in(own, 3), amount)
    donor, sink = mixed[0:amount // 2 * 2:2], mixed[1:amount // 2 * 2:2]
    slack = jnp.minimum(sizes[donor] - 1, most - sizes[sink]) // 2
    slack = jnp.where((donor == sequence[0]) | (sink == sequence[0]) | (sizes[sink] == 0), 0, jnp.maximum(slack, 0))
    shifted = jax.random.randint(jax.random.fold_in(own, 4), (amount // 2,), 0, 1 << 20) % (slack + 1)
    sizes = sizes.at[donor].add(-shifted).at[sink].add(shifted)
    items = jnp.searchsorted(jnp.cumsum(sizes), jnp.arange(rows * top), side="right").astype(jnp.int32)
    grid = items.reshape(top, rows).T
    grid = grid[jax.random.permutation(jax.random.fold_in(own, 1), rows)]
    offset_by = jax.random.randint(jax.random.fold_in(own, 2), (rows, 1), 0, top)
    return jnp.take_along_axis(grid, (jnp.arange(top)[None, :] + offset_by) % top, axis=1)


def load_shares(number_of, total, most, skew, full):
    portions = [(1 << 20) // math.isqrt(grade ** skew) + 1 for grade in range(1, number_of + 1)]
    largest = most if full else min(most, max(-(-total // number_of), total * portions[0] // sum(portions)))
    least = 1 if total - largest >= number_of - 1 else 0
    holding, spare = [largest] + [least] * (number_of - 1), total - largest - least * (number_of - 1)
    while spare > 0:
        free = [i for i in range(1, number_of) if holding[i] < largest] or [i for i in range(1, number_of) if holding[i] < most]
        pool, remaining = sum([portions[i] for i in free]), spare
        for i in free:
            extra = min(most - holding[i], max(1, remaining * portions[i] // pool), spare)
            holding[i] = holding[i] + extra
            spare = spare - extra
    return np.array(holding)


def gaussian(rng, extent, deviation, bound, cuts=(), kind=jnp.bfloat16):
    array = jax.random.normal(rng, extent, jnp.float32) * deviation
    if len(cuts) > 0:
        array = block_levels(rng, extent, cuts, -0.22, 0.18) * array
    return jnp.clip(array, min=-bound, max=bound).astype(kind)


def setup_inputs(seed: int = 0, part: int = 0) -> dict:
    key_list = jax.random.split(jax.random.key(seed), 7)
    part_splits = jax.random.split(jax.random.fold_in(key_list[6], part), 7)
    activations = gaussian(part_splits[0], (TOKENS, D), 1.0, 6.0, ((0, 4), (1, 4)))
    expert_ids_keys = jax.random.split(jax.random.fold_in(part_splits[1], 1), TOKENS // TOK_DEV)
    expert_ids_turns = jax.random.permutation(jax.random.fold_in(part_splits[1], 3), TOKENS // TOK_DEV)
    expert_ids = jax.vmap(lambda own, number: assign_block(jax.random.fold_in(part_splits[1], 2), own, number, TOK_DEV, EXPERTS, TOP, CAP, 2))(expert_ids_keys, expert_ids_turns).reshape((TOKENS, TOP))
    gate_values = jnp.clip(0.2 + 0.8 * jax.random.uniform(part_splits[2], (TOKENS, TOP), jnp.float32) ** block_levels(part_splits[2], (TOKENS, TOP), ((0, 4),), -0.2, 0.2), 0.2, 1.0)
    expert_gate = gaussian(key_list[3], (EXPERTS, D, FF), D ** -0.5, 0.125, ((0, 4), (1, 4)))
    expert_up = gaussian(key_list[4], (EXPERTS, D, FF), D ** -0.5, 0.125, ((0, 4), (1, 4)))
    expert_down = gaussian(key_list[5], (EXPERTS, FF, D), FF ** -0.5, 0.25, ((0, 4), (2, 4)))
    return {"activations": activations, "expert_ids": expert_ids, "gate_values": gate_values, "expert_gate": expert_gate, "expert_up": expert_up, "expert_down": expert_down}


def block_slots(block_ids):
    flat_ids = block_ids.reshape(-1).astype(jnp.int32)
    one_hot = (flat_ids[:, None] == jnp.arange(EXPERTS, dtype=jnp.int32)[None, :]).astype(jnp.int32)
    earlier = jnp.cumsum(one_hot, axis=0) - one_hot
    rank_within = jnp.sum(earlier * one_hot, axis=1)
    return (flat_ids * CAP + rank_within).astype(jnp.int32)


def slice_sum(rows, weights):
    sliced = rows.astype(jnp.float32).reshape(-1, N_TOK, D // N_TOK)
    parted = weights.astype(jnp.float32).reshape(N_TOK, D // N_TOK, FF)
    per_slice = jnp.einsum("rtf,tfh->trh", sliced, parted)
    rounded = lax.optimization_barrier(per_slice.astype(jnp.bfloat16))
    return jnp.sum(rounded.astype(jnp.float32), axis=0)


def expert_rows(inputs):
    rows, gate_w, up_w, down_w = inputs
    hidden = (jax.nn.silu(slice_sum(rows, gate_w)) * slice_sum(rows, up_w)).astype(jnp.bfloat16)
    return jnp.dot(hidden, down_w, preferred_element_type=jnp.float32).astype(jnp.bfloat16)


def reference(activations, expert_ids, gate_values, expert_gate, expert_up, expert_down):
    slots = jax.vmap(block_slots)(expert_ids.reshape(N_EXP, TOK_DEV, TOP))
    picked = jnp.repeat(activations, TOP, axis=0).reshape(N_EXP, TOK_DEV * TOP, D)
    sources = jnp.arange(N_EXP, dtype=jnp.int32)[:, None]
    buffer = jnp.zeros((N_EXP, EXPERTS * CAP, D), jnp.bfloat16).at[sources, slots].set(picked)
    by_expert = buffer.reshape(N_EXP, EXPERTS, CAP, D).transpose(1, 0, 2, 3).reshape(EXPERTS, N_EXP * CAP, D)
    outputs = lax.map(expert_rows, (by_expert, expert_gate, expert_up, expert_down))
    back = outputs.reshape(EXPERTS, N_EXP, CAP, D).transpose(1, 0, 2, 3).reshape(N_EXP, EXPERTS * CAP, D)
    fetched = jnp.take_along_axis(back, slots[:, :, None], axis=1).astype(jnp.float32)
    weighted = fetched.reshape(TOKENS, TOP, D) * gate_values[:, :, None]
    return jnp.sum(weighted, axis=1).astype(jnp.bfloat16)
```

```python
import functools

import jax
import jax.numpy as jnp
from jax import lax
from jax.experimental import pallas as pl
from jax.experimental.pallas import tpu as pltpu
from jax.sharding import PartitionSpec as P

CORES = 2


def slot_positions(expert_ids, experts_all, capacity):
    flat_ids = expert_ids.reshape(-1)
    one_hot = (flat_ids[:, None] == jnp.arange(experts_all, dtype=jnp.int32)[None, :]).astype(
        jnp.int32
    )
    earlier = jnp.cumsum(one_hot, axis=0) - one_hot
    rank_within = jnp.sum(earlier * one_hot, axis=1)
    return flat_ids * capacity + rank_within


def move_rows(buffer):
    return lax.all_to_all(buffer, "exp", split_axis=0, concat_axis=0, tiled=True)


def slot_plan(activations, expert_ids, gate_values, expert_gate, expert_up, expert_down, capacity):
    row_count, feature_cols = activations.shape
    top_count = expert_ids.shape[1]
    local_experts = expert_gate.shape[0]
    groups = lax.axis_size("exp")
    experts_all = local_experts * groups
    slot_index = slot_positions(expert_ids, experts_all, capacity)
    picked = jnp.repeat(activations, top_count, axis=0)
    outgoing = (
        jnp.zeros((experts_all * capacity, feature_cols), jnp.bfloat16).at[slot_index].set(picked)
    )
    arrived = move_rows(outgoing.reshape(groups, local_experts, capacity, feature_cols))
    gate_part = jnp.einsum(
        "sxcf,xfh->sxch", arrived, expert_gate, preferred_element_type=jnp.float32
    )
    up_part = jnp.einsum("sxcf,xfh->sxch", arrived, expert_up, preferred_element_type=jnp.float32)
    gate_pre, up_pre = (
        lax.psum(gate_part.astype(jnp.bfloat16), "tok").astype(jnp.float32),
        lax.psum(up_part.astype(jnp.bfloat16), "tok").astype(jnp.float32),
    )
    hidden = (jax.nn.silu(gate_pre) * up_pre).astype(jnp.bfloat16)
    results = jnp.einsum(
        "sxch,xhf->sxcf", hidden, expert_down, preferred_element_type=jnp.float32
    ).astype(jnp.bfloat16)
    returned = move_rows(results).reshape(experts_all * capacity, feature_cols)
    fetched = returned[slot_index].astype(jnp.float32).reshape(row_count, top_count, feature_cols)
    combined = jnp.sum(fetched * gate_values[:, :, None], axis=1)
    return combined.astype(jnp.bfloat16)


VMEM = pl.BlockSpec(memory_space=pltpu.VMEM)
LANES = 128


def call(kernel, out_shape, *operands):
    return pl.pallas_call(
        kernel,
        out_shape=out_shape,
        in_specs=[VMEM] * len(operands),
        out_specs=jax.tree.map(lambda _: VMEM, out_shape),
        compiler_params=pltpu.CompilerParams(vmem_limit_bytes=32 * 1024 * 1024),
        cost_estimate=pl.CostEstimate(flops=1, bytes_accessed=1, transcendentals=0),
    )(*operands)


def dot(rows, weights):
    return jnp.dot(rows, weights, preferred_element_type=jnp.float32)


def share(core, rows):
    return pl.ds(pl.multiple_of(core * rows, rows), rows)


def pack_kernel(own_ref, other_ref, ids_ref, gates_ref, out_ref, *, experts_all):
    rows, cols = out_ref.shape[0], own_ref.shape[1]
    mine = share(lax.axis_index("tok") % CORES, rows)
    out_ref[:, :cols] = own_ref[mine, :]
    out_ref[:, cols : 2 * cols] = other_ref[mine, :]
    ids, gates = ids_ref[mine, :], gates_ref[mine, :]
    lane = lax.broadcasted_iota(jnp.int32, (rows, out_ref.shape[1] - 2 * cols), 1)
    expert = lax.rem(lane, experts_all)
    weight = jnp.zeros(lane.shape, jnp.float32)
    for k in range(ids.shape[1]):
        weight += jnp.where(ids[:, k : k + 1] == expert, gates[:, k : k + 1], 0.0)
    high = weight.astype(jnp.bfloat16)
    low = (weight - high.astype(jnp.float32)).astype(jnp.bfloat16)
    out_ref[:, 2 * cols :] = jnp.where(lane < experts_all, high, low)


def part_kernel(message_ref, gate_ref, other_gate_ref, up_ref, other_up_ref, out_ref):
    cols = gate_ref.shape[1]
    own, other = message_ref[:, :cols], message_ref[:, cols : 2 * cols]
    for i, (own_ref, other_ref) in enumerate(
        ((gate_ref, other_gate_ref), (up_ref, other_up_ref))
    ):
        for x in range(gate_ref.shape[0]):
            product = dot(own, own_ref[x]) + dot(other, other_ref[x])
            out_ref[i, x] = product.astype(out_ref.dtype)


def down_kernel(message_ref, down_ref, other_down_ref, *refs, experts_all):
    parts, out_ref = refs[:-1], refs[-1]
    local_experts, _, cols = down_ref.shape
    first = lax.axis_index("exp") * local_experts
    table = message_ref[:, 2 * cols :].astype(jnp.float32)
    lane = lax.broadcasted_iota(jnp.int32, table.shape, 1)
    own, other = 0.0, 0.0
    for x in range(local_experts):
        chosen = (lane == first + x) | (lane == first + x + experts_all)
        weight = jnp.sum(jnp.where(chosen, table, 0.0), axis=1, keepdims=True)
        gate = sum(part[0, x].astype(jnp.float32) for part in parts)
        up = sum(part[1, x].astype(jnp.float32) for part in parts)
        hidden = (gate / (1.0 + jnp.exp(-gate)) * up * weight).astype(jnp.bfloat16)
        own += dot(hidden, down_ref[x])
        other += dot(hidden, other_down_ref[x])
    out_ref[:, :cols] = own.astype(out_ref.dtype)
    out_ref[:, cols:] = other.astype(out_ref.dtype)


def total_kernel(*refs):
    results, keep_ref, send_ref = refs[:-2], refs[-2], refs[-1]
    cols = keep_ref.shape[1]
    for out_ref, part in ((keep_ref, slice(0, cols)), (send_ref, slice(cols, None))):
        total = sum(result[:, part].astype(jnp.float32) for result in results)
        out_ref[...] = total.astype(out_ref.dtype)


def place_kernel(keep_ref, taken_ref, out_ref):
    core, rows = lax.axis_index("tok") % CORES, keep_ref.shape[0]
    out_ref[share(core, rows), :] = keep_ref[...]
    out_ref[share(1 - core, rows), :] = taken_ref[...]


def exchange(array, axis, distance):
    return lax.ppermute(
        array, axis, [(i, i ^ distance) for i in range(lax.axis_size(axis))]
    )


def after(array, *ready):
    return lax.optimization_barrier((array, *ready))[0] if ready else array


def dense_plan(activations, expert_ids, gate_values, expert_gate, expert_up, expert_down):
    row_count, feature_cols = activations.shape
    local_experts, _, hidden_cols = expert_gate.shape
    groups = lax.axis_size("exp")
    chips = lax.axis_size("tok") // CORES
    experts_all = local_experts * groups
    rows = row_count // CORES
    table_cols = -(-2 * experts_all // LANES) * LANES

    other_rows = exchange(activations, "tok", 1)
    gate, up, down = (
        (own, exchange(own, "tok", 1)) for own in (expert_gate, expert_up, expert_down)
    )
    message = call(
        functools.partial(pack_kernel, experts_all=experts_all),
        jax.ShapeDtypeStruct((rows, 2 * feature_cols + table_cols), jnp.bfloat16),
        activations,
        other_rows,
        expert_ids,
        gate_values,
    )
    messages = {0: message}
    distance = groups // 2
    while distance:
        for step in list(messages):
            messages[step ^ distance] = exchange(messages[step], "exp", distance)
        distance //= 2

    done = []

    def held_back(array):
        return after(array, *done[-1:])

    def multiply(step):
        part = call(
            part_kernel,
            jax.ShapeDtypeStruct((2, local_experts, rows, hidden_cols), jnp.bfloat16),
            held_back(messages[step]),
            *gate,
            *up,
        )
        done.append(part)
        return [part] + [exchange(part, "tok", chip * CORES) for chip in range(1, chips)]

    def finish(step, parts):
        result = call(
            functools.partial(down_kernel, experts_all=experts_all),
            jax.ShapeDtypeStruct(
                (rows, 2 * feature_cols), jnp.bfloat16 if step else jnp.float32
            ),
            messages[step],
            *down,
            held_back(parts[0]),
            *parts[1:],
        )
        done.append(result)
        return exchange(result, "exp", step) if step else result

    order = [*range(1, groups), 0]
    ahead = groups // 2
    parts = {step: multiply(step) for step in order[:ahead]}
    results = []
    for i, step in enumerate(order):
        results.append(finish(step, parts[step]))
        for other in order[ahead + i : ahead + i + 1]:
            parts[other] = multiply(other)
    keep, send = call(
        total_kernel,
        [jax.ShapeDtypeStruct((rows, feature_cols), jnp.bfloat16)] * 2,
        *results,
    )
    return call(
        place_kernel,
        jax.ShapeDtypeStruct((row_count, feature_cols), jnp.bfloat16),
        keep,
        exchange(send, "tok", 1),
    )


def shards(activations, expert_ids, gate_values, expert_gate, expert_up, expert_down):
    row_count = activations.shape[0]
    local_experts = expert_gate.shape[0]
    groups, pieces = lax.axis_size("exp"), lax.axis_size("tok")
    capacity = 2 * row_count * expert_ids.shape[1] // (local_experts * groups)
    arrays = (activations, expert_ids, gate_values, expert_gate, expert_up, expert_down)
    paired = groups & (groups - 1) == 0 and pieces & (pieces - 1) == 0 and pieces >= CORES
    if capacity >= row_count and row_count % (16 * CORES) == 0 and paired:
        return dense_plan(*arrays)
    return slot_plan(*arrays, capacity)


def solution(mesh):
    placed = (
        P(("group", "exp"), "tok"),
        P(("group", "exp"), None),
        P(("group", "exp"), None),
        P("exp", "tok", None),
        P("exp", "tok", None),
        P("exp", None, "tok"),
    )
    return jax.shard_map(
        shards, mesh=mesh, in_specs=placed, out_specs=P(("group", "exp"), "tok"), check_vma=False
    )
```

```python
import functools

import jax
import jax.numpy as jnp
from jax import lax
from jax.experimental import pallas as pl
from jax.experimental.pallas import tpu as pltpu
from jax.sharding import PartitionSpec as P

CORES = 2


def slot_positions(expert_ids, experts_all, capacity):
    flat_ids = expert_ids.reshape(-1)
    one_hot = (flat_ids[:, None] == jnp.arange(experts_all, dtype=jnp.int32)[None, :]).astype(
        jnp.int32
    )
    earlier = jnp.cumsum(one_hot, axis=0) - one_hot
    rank_within = jnp.sum(earlier * one_hot, axis=1)
    return flat_ids * capacity + rank_within


def move_rows(buffer):
    return lax.all_to_all(buffer, "exp", split_axis=0, concat_axis=0, tiled=True)


def slot_plan(activations, expert_ids, gate_values, expert_gate, expert_up, expert_down, capacity):
    row_count, feature_cols = activations.shape
    top_count = expert_ids.shape[1]
    local_experts = expert_gate.shape[0]
    groups = lax.axis_size("exp")
    experts_all = local_experts * groups
    slot_index = slot_positions(expert_ids, experts_all, capacity)
    picked = jnp.repeat(activations, top_count, axis=0)
    outgoing = (
        jnp.zeros((experts_all * capacity, feature_cols), jnp.bfloat16).at[slot_index].set(picked)
    )
    arrived = move_rows(outgoing.reshape(groups, local_experts, capacity, feature_cols))
    gate_part = jnp.einsum(
        "sxcf,xfh->sxch", arrived, expert_gate, preferred_element_type=jnp.float32
    )
    up_part = jnp.einsum("sxcf,xfh->sxch", arrived, expert_up, preferred_element_type=jnp.float32)
    gate_pre, up_pre = (
        lax.psum(gate_part.astype(jnp.bfloat16), "tok").astype(jnp.float32),
        lax.psum(up_part.astype(jnp.bfloat16), "tok").astype(jnp.float32),
    )
    hidden = (jax.nn.silu(gate_pre) * up_pre).astype(jnp.bfloat16)
    results = jnp.einsum(
        "sxch,xhf->sxcf", hidden, expert_down, preferred_element_type=jnp.float32
    ).astype(jnp.bfloat16)
    returned = move_rows(results).reshape(experts_all * capacity, feature_cols)
    fetched = returned[slot_index].astype(jnp.float32).reshape(row_count, top_count, feature_cols)
    combined = jnp.sum(fetched * gate_values[:, :, None], axis=1)
    return combined.astype(jnp.bfloat16)


VMEM = pl.BlockSpec(memory_space=pltpu.VMEM)
LANES = 128


def call(kernel, out_shape, *operands, scratch=()):
    return pl.pallas_call(
        kernel,
        out_shape=out_shape,
        in_specs=[VMEM] * len(operands),
        out_specs=jax.tree.map(lambda _: VMEM, out_shape),
        scratch_shapes=scratch,
        compiler_params=pltpu.CompilerParams(vmem_limit_bytes=16 * 1024 * 1024),
        cost_estimate=pl.CostEstimate(flops=1, bytes_accessed=1, transcendentals=0),
    )(*operands)


class Chain:
    def __init__(self):
        self.token = None

    def call(self, kernel, out_shape, *operands, scratch=()):
        count = len(operands)
        ahead = () if self.token is None else (self.token,)

        def chained(*refs):
            token_ref, outs = refs[count + len(ahead)], refs[count + len(ahead) + 1 :]
            token_ref[...] = jnp.zeros_like(token_ref)
            kernel(*refs[:count], *outs)

        token = jax.ShapeDtypeStruct((8, LANES), jnp.float32)
        self.token, *results = call(
            chained, [token, *out_shape], *operands, *ahead, scratch=scratch
        )
        return results


def dot(rows, weights):
    return jnp.dot(rows, weights, preferred_element_type=jnp.float32)


def share(core, rows):
    return pl.ds(pl.multiple_of(core * rows, rows), rows)


def pack_kernel(own_ref, other_ref, weights_ref, out_ref, table_ref):
    rows, cols = out_ref.shape[0], own_ref.shape[1]
    mine = share(lax.axis_index("tok") % CORES, rows)
    out_ref[:, :cols] = own_ref[mine, :]
    out_ref[:, cols : 2 * cols] = other_ref[mine, :]
    weights = weights_ref[...]
    high = weights.astype(jnp.bfloat16).astype(jnp.float32)
    table = jnp.concatenate([high, weights - high])
    table_ref[...] = jnp.zeros_like(table_ref)
    table_ref[:, : table.shape[0]] = table.T
    out_ref[:, 2 * cols :] = table_ref[mine, :].astype(jnp.bfloat16)


def part_kernel(
    message_ref, gate_ref, other_gate_ref, up_ref, other_up_ref, *outs, first
):
    cols = gate_ref.shape[1]
    gate_out, up_out = outs if len(outs) > 1 else (outs[0].at[0], outs[0].at[1])
    taken = slice(first, first + gate_out.shape[1])
    own, other = message_ref[taken, :cols], message_ref[taken, cols : 2 * cols]
    for own_ref, other_ref, out_ref in (
        (gate_ref, other_gate_ref, gate_out),
        (up_ref, other_up_ref, up_out),
    ):
        for x in range(gate_ref.shape[0]):
            product = dot(own, own_ref[x]) + dot(other, other_ref[x])
            out_ref[x] = product.astype(out_ref.dtype)


def down_kernel(message_ref, down_ref, other_down_ref, *refs, first_row, experts_all):
    parts, out_ref = refs[:-1], refs[-1]
    local_experts, _, cols = down_ref.shape
    first = lax.axis_index("exp") * local_experts
    taken = slice(first_row, first_row + out_ref.shape[0])
    table = message_ref[taken, 2 * cols :].astype(jnp.float32)
    lane = lax.broadcasted_iota(jnp.int32, table.shape, 1)
    own, other = 0.0, 0.0
    for x in range(local_experts):
        chosen = (lane == first + x) | (lane == first + x + experts_all)
        weight = jnp.sum(jnp.where(chosen, table, 0.0), axis=1, keepdims=True)
        if len(parts[0].shape) == 4:
            gate = sum(part[0, x].astype(jnp.float32) for part in parts)
            up = sum(part[1, x].astype(jnp.float32) for part in parts)
        else:
            gate = sum(part[x].astype(jnp.float32) for part in parts[0::2])
            up = sum(part[x].astype(jnp.float32) for part in parts[1::2])
        hidden = (gate / (1.0 + jnp.exp(-gate)) * up * weight).astype(jnp.bfloat16)
        own += dot(hidden, down_ref[x])
        other += dot(hidden, other_down_ref[x])
    out_ref[:, :cols] = own.astype(out_ref.dtype)
    out_ref[:, cols:] = other.astype(out_ref.dtype)


def total_kernel(*refs, rows):
    keep_ref, send_ref = refs[-2:]
    cols = keep_ref.shape[1]
    for out_ref, part in ((keep_ref, slice(0, cols)), (send_ref, slice(cols, None))):
        for first, last, results in rows:
            total = sum(
                refs[i][slice(first - start, last - start), part].astype(jnp.float32)
                for i, start in results
            )
            out_ref[first:last, :] = total.astype(out_ref.dtype)


def place_kernel(keep_ref, taken_ref, out_ref):
    core, rows = lax.axis_index("tok") % CORES, keep_ref.shape[0]
    out_ref[share(core, rows), :] = keep_ref[...]
    out_ref[share(1 - core, rows), :] = taken_ref[...]


def exchange(array, axis, distance):
    return lax.ppermute(
        array, axis, [(i, i ^ distance) for i in range(lax.axis_size(axis))]
    )


def after(array, *ready):
    return lax.optimization_barrier((array, *ready))[0] if ready else array


def dense_plan(activations, expert_ids, gate_values, expert_gate, expert_up, expert_down):
    row_count, feature_cols = activations.shape
    local_experts, _, hidden_cols = expert_gate.shape
    groups = lax.axis_size("exp")
    chips = lax.axis_size("tok") // CORES
    experts_all = local_experts * groups
    rows = row_count // CORES
    table_cols = -(-2 * experts_all // LANES) * LANES

    other_rows = exchange(activations, "tok", 1)
    named = expert_ids[None, :, :] == jnp.arange(experts_all, dtype=jnp.int32)[:, None, None]
    weights = jnp.sum(jnp.where(named, gate_values[None], 0.0), axis=2)
    chain = Chain()
    (message,) = chain.call(
        pack_kernel,
        [jax.ShapeDtypeStruct((rows, 2 * feature_cols + table_cols), jnp.bfloat16)],
        activations,
        other_rows,
        weights,
        scratch=[pltpu.VMEM((row_count, table_cols), jnp.float32)],
    )
    gate, up, down = (
        (own, exchange(after(own, other_rows), "tok", 1))
        for own in (expert_gate, expert_up, expert_down)
    )
    messages = {0: message}
    for step in range(1, groups):
        messages[step] = exchange(message, "exp", step)
    parts, results = {}, {}

    def multiply(job):
        step, first, last = job
        shape = (local_experts, last - first, hidden_cols)
        shapes = [shape, shape] if job != order[0] else [(2, *shape)]
        pair = chain.call(
            functools.partial(part_kernel, first=first),
            [jax.ShapeDtypeStruct(shape, jnp.bfloat16) for shape in shapes],
            messages[step],
            *gate,
            *up,
        )
        parts[job] = [*pair]
        for chip in range(1, chips):
            parts[job] += [exchange(part, "tok", chip * CORES) for part in pair]

    def finish(job):
        step, first, last = job
        dtype = jnp.bfloat16 if step else jnp.float32
        (result,) = (call if job == order[-1] else chain.call)(
            functools.partial(down_kernel, first_row=first, experts_all=experts_all),
            [jax.ShapeDtypeStruct((last - first, 2 * feature_cols), dtype)],
            messages[step],
            *down,
            *parts[job],
        )
        results[job] = exchange(result, "exp", step) if step else result

    half = rows // 2
    order = [(0,0,rows),(2,0,rows),(3,0,rows),(1,0,rows)]
    ahead = groups // 2
    for job in order[:ahead]:
        multiply(job)
    for i, job in enumerate(order):
        finish(job)
        for later in order[ahead + i : ahead + i + 1]:
            multiply(later)
    jobs = list(results)
    spans = [
        (
            lo,
            lo + half,
            [(i, first) for i, (_, first, last) in enumerate(jobs) if first <= lo < last],
        )
        for lo in range(0, rows, half)
    ]
    keep, send = call(
        functools.partial(total_kernel, rows=spans),
        [jax.ShapeDtypeStruct((rows, feature_cols), jnp.bfloat16)] * 2,
        *results.values(),
    )
    return call(
        place_kernel,
        jax.ShapeDtypeStruct((row_count, feature_cols), jnp.bfloat16),
        keep,
        exchange(send, "tok", 1),
    )


def shards(activations, expert_ids, gate_values, expert_gate, expert_up, expert_down):
    row_count = activations.shape[0]
    local_experts = expert_gate.shape[0]
    groups, pieces = lax.axis_size("exp"), lax.axis_size("tok")
    capacity = 2 * row_count * expert_ids.shape[1] // (local_experts * groups)
    arrays = (activations, expert_ids, gate_values, expert_gate, expert_up, expert_down)
    paired = groups & (groups - 1) == 0 and pieces & (pieces - 1) == 0 and pieces >= CORES
    if capacity >= row_count and row_count % (16 * CORES) == 0 and paired:
        return dense_plan(*arrays)
    return slot_plan(*arrays, capacity)


def solution(mesh):
    placed = (
        P(("group", "exp"), "tok"),
        P(("group", "exp"), None),
        P(("group", "exp"), None),
        P("exp", "tok", None),
        P("exp", "tok", None),
        P("exp", None, "tok"),
    )
    return jax.shard_map(
        shards, mesh=mesh, in_specs=placed, out_specs=P(("group", "exp"), "tok"), check_vma=False
    )
```

```python
import functools
import math

import jax
import jax.numpy as jnp
import numpy as np
from jax import lax
from jax.experimental import pallas as pl
from jax.experimental.pallas import tpu as pltpu
from jax.sharding import PartitionSpec as P

CORES = 2


def slot_positions(expert_ids, experts_all, capacity):
    flat_ids = expert_ids.reshape(-1)
    one_hot = (flat_ids[:, None] == jnp.arange(experts_all, dtype=jnp.int32)[None, :]).astype(
        jnp.int32
    )
    earlier = jnp.cumsum(one_hot, axis=0) - one_hot
    rank_within = jnp.sum(earlier * one_hot, axis=1)
    return flat_ids * capacity + rank_within


def move_rows(buffer):
    return lax.all_to_all(buffer, "exp", split_axis=0, concat_axis=0, tiled=True)


def slot_plan(activations, expert_ids, gate_values, expert_gate, expert_up, expert_down, capacity):
    row_count, feature_cols = activations.shape
    top_count = expert_ids.shape[1]
    local_experts = expert_gate.shape[0]
    groups = lax.axis_size("exp")
    experts_all = local_experts * groups
    slot_index = slot_positions(expert_ids, experts_all, capacity)
    picked = jnp.repeat(activations, top_count, axis=0)
    outgoing = (
        jnp.zeros((experts_all * capacity, feature_cols), jnp.bfloat16).at[slot_index].set(picked)
    )
    arrived = move_rows(outgoing.reshape(groups, local_experts, capacity, feature_cols))
    gate_part = jnp.einsum(
        "sxcf,xfh->sxch", arrived, expert_gate, preferred_element_type=jnp.float32
    )
    up_part = jnp.einsum("sxcf,xfh->sxch", arrived, expert_up, preferred_element_type=jnp.float32)
    gate_pre, up_pre = (
        lax.psum(gate_part.astype(jnp.bfloat16), "tok").astype(jnp.float32),
        lax.psum(up_part.astype(jnp.bfloat16), "tok").astype(jnp.float32),
    )
    hidden = (jax.nn.silu(gate_pre) * up_pre).astype(jnp.bfloat16)
    results = jnp.einsum(
        "sxch,xhf->sxcf", hidden, expert_down, preferred_element_type=jnp.float32
    ).astype(jnp.bfloat16)
    returned = move_rows(results).reshape(experts_all * capacity, feature_cols)
    fetched = returned[slot_index].astype(jnp.float32).reshape(row_count, top_count, feature_cols)
    combined = jnp.sum(fetched * gate_values[:, :, None], axis=1)
    return combined.astype(jnp.bfloat16)


VMEM = pl.BlockSpec(memory_space=pltpu.VMEM)
LEFT = pl.BlockSpec(memory_space=pltpu.HBM)
LANES = 128


def call(kernel, out_shape, *operands, scratch=(), left=()):
    operands = [
        pltpu.with_memory_space_constraint(a, pltpu.HBM) if i in left else a
        for i, a in enumerate(operands)
    ]
    return pl.pallas_call(
        kernel,
        out_shape=out_shape,
        in_specs=[LEFT if i in left else VMEM for i in range(len(operands))],
        out_specs=jax.tree.map(lambda _: VMEM, out_shape),
        scratch_shapes=scratch,
        compiler_params=pltpu.CompilerParams(vmem_limit_bytes=16 * 1024 * 1024),
        cost_estimate=pl.CostEstimate(flops=1, bytes_accessed=1, transcendentals=0),
    )(*operands)


class Chain:
    def __init__(self):
        self.token = None

    def call(self, kernel, out_shape, *operands, scratch=(), left=(), last=False):
        count = len(operands)
        ahead = () if self.token is None else (self.token,)

        def ended(*refs):
            kernel(*refs[:count], *refs[count + len(ahead) :])

        if last:
            return call(ended, out_shape, *operands, *ahead, scratch=scratch, left=left)

        def chained(*refs):
            token_ref, outs = refs[count + len(ahead)], refs[count + len(ahead) + 1 :]
            token_ref[...] = jnp.zeros_like(token_ref)
            kernel(*refs[:count], *outs)

        token = jax.ShapeDtypeStruct((8, LANES), jnp.float32)
        self.token, *results = call(
            chained, [token, *out_shape], *operands, *ahead, scratch=scratch, left=left
        )
        return results


def dot(rows, weights):
    return jnp.dot(rows, weights, preferred_element_type=jnp.float32)


def share(core, rows):
    return pl.ds(pl.multiple_of(core * rows, rows), rows)


def pack_kernel(
    own_ref, other_ref, ids_ref, gates_ref, out_ref, ids_mine, gates_mine, table_ref, sems, *,
    experts_all
):
    rows, cols = out_ref.shape[0], own_ref.shape[1]
    mine = share(lax.axis_index("tok") % CORES, rows)
    copies = [
        pltpu.make_async_copy(source, target, sems.at[i])
        for i, (source, target) in enumerate(
            (
                (ids_ref, ids_mine),
                (gates_ref, gates_mine),
                (own_ref.at[mine, :], out_ref.at[:, pl.ds(0, cols)]),
            )
        )
    ]
    for copy in copies:
        copy.start()
    out_ref[:, cols : 2 * cols] = other_ref[mine, :]
    copies[0].wait()
    copies[1].wait()
    line = lax.broadcasted_iota(jnp.int32, (2 * experts_all, table_ref.shape[0]), 0)
    expert = lax.rem(line, experts_all)
    weight = jnp.zeros(line.shape, jnp.float32)
    for k in range(ids_mine.shape[0]):
        weight += jnp.where(ids_mine[k : k + 1, :] == expert, gates_mine[k : k + 1, :], 0.0)
    high = weight.astype(jnp.bfloat16).astype(jnp.float32)
    table_ref[...] = jnp.zeros_like(table_ref)
    table_ref[:, : 2 * experts_all] = jnp.where(line < experts_all, high, weight - high).T
    out_ref[:, 2 * cols :] = table_ref[mine, :].astype(jnp.bfloat16)
    copies[2].wait()


def first_part_kernel(
    message_ref, gate_ref, other_gate_ref, up_ref, other_up_ref, out_ref, gate_out, up_out, sems
):
    cols = gate_ref.shape[1]
    copies = [
        pltpu.make_async_copy(source.at[x], target.at[x], sems.at[i, x])
        for i, (source, target) in enumerate(((gate_ref, gate_out), (up_ref, up_out)))
        for x in range(gate_ref.shape[0])
    ]
    for copy in copies:
        copy.start()
    own, other = message_ref[:, :cols], message_ref[:, cols : 2 * cols]
    places = [(i, x) for i in range(2) for x in range(gate_ref.shape[0])]
    products = [dot(other, (other_gate_ref, other_up_ref)[i][x]) for i, x in places]
    for (i, x), copy, product in zip(places, copies, products, strict=True):
        copy.wait()
        product += dot(own, (gate_out, up_out)[i][x])
        out_ref[i, x] = product.astype(out_ref.dtype)


def part_kernel(message_ref, gate_ref, other_gate_ref, up_ref, other_up_ref, *outs):
    cols = gate_ref.shape[1]
    gate_out, up_out = outs if len(outs) > 1 else (outs[0].at[0], outs[0].at[1])
    own, other = message_ref[:, :cols], message_ref[:, cols : 2 * cols]
    for own_ref, other_ref, out_ref in (
        (gate_ref, other_gate_ref, gate_out),
        (up_ref, other_up_ref, up_out),
    ):
        for x in range(gate_ref.shape[0]):
            product = dot(own, own_ref[x]) + dot(other, other_ref[x])
            out_ref[x] = product.astype(out_ref.dtype)


def down_kernel(message_ref, down_ref, other_down_ref, *refs, count, experts_all):
    parts = refs[:count]
    *_, out_ref = outs = refs[count:]
    local_experts, _, cols = down_ref.shape
    first = lax.axis_index("exp") * local_experts
    table = message_ref[:, 2 * cols :].astype(jnp.float32)
    lane = lax.broadcasted_iota(jnp.int32, table.shape, 1)
    own, other = 0.0, 0.0
    for x in range(local_experts):
        chosen = (lane == first + x) | (lane == first + x + experts_all)
        weight = jnp.sum(jnp.where(chosen, table, 0.0), axis=1, keepdims=True)
        if len(parts[0].shape) == 4:
            gate = sum(part[0, x].astype(jnp.float32) for part in parts)
            up = sum(part[1, x].astype(jnp.float32) for part in parts)
        else:
            gate = sum(part[x].astype(jnp.float32) for part in parts[0::2])
            up = sum(part[x].astype(jnp.float32) for part in parts[1::2])
        hidden = (gate / (1.0 + jnp.exp(-gate)) * up * weight).astype(jnp.bfloat16)
        own += dot(hidden, down_ref[x])
        other += dot(hidden, other_down_ref[x])
    own_ref, other_ref = outs if len(outs) > 1 else (out_ref.at[:, :cols], out_ref.at[:, cols:])
    own_ref[...] = own.astype(out_ref.dtype)
    other_ref[...] = other.astype(out_ref.dtype)


def total_kernel(*refs):
    results, (keep_ref, send_ref) = refs[:-2], refs[-2:]
    cols = keep_ref.shape[1]
    for out_ref, part in ((keep_ref, slice(0, cols)), (send_ref, slice(cols, None))):
        total = sum(result[:, part].astype(jnp.float32) for result in results)
        out_ref[...] = total.astype(out_ref.dtype)


def place_kernel(keep_ref, taken_ref, last_keep_ref, last_taken_ref, out_ref):
    core, rows = lax.axis_index("tok") % CORES, keep_ref.shape[0]
    kept = keep_ref[...] + last_keep_ref[...].astype(jnp.float32)
    taken = taken_ref[...] + last_taken_ref[...].astype(jnp.float32)
    out_ref[share(core, rows), :] = kept.astype(out_ref.dtype)
    out_ref[share(1 - core, rows), :] = taken.astype(out_ref.dtype)


def exchange(array, axes, distance):
    if isinstance(axes, str):
        axes, distance = (axes,), (distance,)
    indices = np.arange(math.prod(map(lax.axis_size, axes))).reshape([*map(lax.axis_size, axes)])
    others = indices[np.ix_(*(np.arange(n) ^ d for n, d in zip(indices.shape, distance)))]
    pairs = zip(indices.ravel().tolist(), others.ravel().tolist(), strict=True)
    return lax.ppermute(array, axes, list(pairs))


def after(array, *ready):
    return lax.optimization_barrier((array, *ready))[0] if ready else array


def dense_plan(activations, expert_ids, gate_values, expert_gate, expert_up, expert_down):
    row_count, feature_cols = activations.shape
    local_experts, _, hidden_cols = expert_gate.shape
    groups = lax.axis_size("exp")
    chips = lax.axis_size("tok") // CORES
    experts_all = local_experts * groups
    rows = row_count // CORES
    table_cols = -(-2 * experts_all // LANES) * LANES

    other_rows = exchange(activations, "tok", 1)
    chain = Chain()
    (message,) = chain.call(
        functools.partial(pack_kernel, experts_all=experts_all),
        [jax.ShapeDtypeStruct((rows, 2 * feature_cols + table_cols), jnp.bfloat16)],
        activations,
        other_rows,
        expert_ids.T,
        gate_values.T,
        scratch=[
            pltpu.VMEM(expert_ids.shape[::-1], jnp.int32),
            pltpu.VMEM(gate_values.shape[::-1], jnp.float32),
            pltpu.VMEM((row_count, table_cols), jnp.float32),
            pltpu.SemaphoreType.DMA((3,)),
        ],
        left=(0, 2, 3),
    )
    gate, up, down = (
        [own, exchange(after(own, other_rows), "tok", 1)]
        for own in (expert_gate, expert_up, expert_down)
    )
    messages = {0: message}
    distance = groups // 2
    while distance:
        for step in list(messages):
            messages[step ^ distance] = exchange(messages[step], "exp", distance)
        distance //= 2
    parts, results = {}, {}

    def multiply(step):
        if not parts:
            shape = jax.ShapeDtypeStruct((2, local_experts, rows, hidden_cols), jnp.bfloat16)
            own = [jax.ShapeDtypeStruct(w.shape, w.dtype) for w in (expert_gate, expert_up)]
            part, gate[0], up[0] = chain.call(
                first_part_kernel,
                [shape, *own],
                messages[step],
                *gate,
                *up,
                scratch=[pltpu.SemaphoreType.DMA((2, local_experts))],
                left=(1, 3),
            )
            parts[step] = [part] + [
                exchange(part, "tok", chip * CORES) for chip in range(1, chips)
            ]
            return
        shape = (local_experts, rows, hidden_cols)
        shapes = [(2, *shape)] if step != order[1] else [shape, shape]
        pair = chain.call(
            part_kernel,
            [jax.ShapeDtypeStruct(shape, jnp.bfloat16) for shape in shapes],
            messages[step],
            *gate,
            *up,
        )
        parts[step] = [*pair]
        for chip in range(1, chips):
            parts[step] += [exchange(part, "tok", chip * CORES) for part in pair]

    def finish(step):
        dtype = jnp.bfloat16 if step else jnp.float32
        pieces = 2 if step == order[-1] else 1
        shape = jax.ShapeDtypeStruct((rows, 2 * feature_cols // pieces), dtype)
        result = chain.call(
            functools.partial(
                down_kernel, count=len(parts[step]), experts_all=experts_all
            ),
            [shape] * pieces,
            messages[step],
            *down,
            *parts[step],
            last=pieces == 2,
        )
        if pieces == 2:
            results[step] = (
                exchange(result[0], "exp", step),
                exchange(result[1], ("exp", "tok"), (step, 1)),
            )
        else:
            results[step] = exchange(result[0], "exp", step) if step else result[0]

    order = [0, *range(2, groups), 1]
    ahead = groups // 2
    for step in order[:ahead]:
        multiply(step)
    for i, step in enumerate(order):
        finish(step)
        for later in order[ahead + i : ahead + i + 1]:
            multiply(later)
    last_keep, last_taken = results.pop(order[-1])
    keep, send = call(
        total_kernel,
        [
            jax.ShapeDtypeStruct((rows, feature_cols), jnp.float32),
            jax.ShapeDtypeStruct((rows, feature_cols), jnp.bfloat16),
        ],
        *results.values(),
    )
    return call(
        place_kernel,
        jax.ShapeDtypeStruct((row_count, feature_cols), jnp.bfloat16),
        keep,
        exchange(send, "tok", 1),
        last_keep,
        last_taken,
    )


def shards(activations, expert_ids, gate_values, expert_gate, expert_up, expert_down):
    row_count = activations.shape[0]
    local_experts = expert_gate.shape[0]
    groups, pieces = lax.axis_size("exp"), lax.axis_size("tok")
    capacity = 2 * row_count * expert_ids.shape[1] // (local_experts * groups)
    arrays = (activations, expert_ids, gate_values, expert_gate, expert_up, expert_down)
    paired = groups & (groups - 1) == 0 and pieces & (pieces - 1) == 0 and pieces >= CORES
    if capacity >= row_count and row_count % (16 * CORES) == 0 and paired:
        return dense_plan(*arrays)
    return slot_plan(*arrays, capacity)


def solution(mesh):
    placed = (
        P(("group", "exp"), "tok"),
        P(("group", "exp"), None),
        P(("group", "exp"), None),
        P("exp", "tok", None),
        P("exp", "tok", None),
        P("exp", None, "tok"),
    )
    return jax.shard_map(
        shards, mesh=mesh, in_specs=placed, out_specs=P(("group", "exp"), "tok"), check_vma=False
    )
```

```python
import functools
import math

import jax
import jax.numpy as jnp
import numpy as np
from jax import lax
from jax.experimental import pallas as pl
from jax.experimental.pallas import tpu as pltpu
from jax.sharding import PartitionSpec as P

CORES = 2


def slot_positions(expert_ids, experts_all, capacity):
    flat_ids = expert_ids.reshape(-1)
    one_hot = (flat_ids[:, None] == jnp.arange(experts_all, dtype=jnp.int32)[None, :]).astype(
        jnp.int32
    )
    earlier = jnp.cumsum(one_hot, axis=0) - one_hot
    rank_within = jnp.sum(earlier * one_hot, axis=1)
    return flat_ids * capacity + rank_within


def move_rows(buffer):
    return lax.all_to_all(buffer, "exp", split_axis=0, concat_axis=0, tiled=True)


def slot_plan(activations, expert_ids, gate_values, expert_gate, expert_up, expert_down, capacity):
    row_count, feature_cols = activations.shape
    top_count = expert_ids.shape[1]
    local_experts = expert_gate.shape[0]
    groups = lax.axis_size("exp")
    experts_all = local_experts * groups
    slot_index = slot_positions(expert_ids, experts_all, capacity)
    picked = jnp.repeat(activations, top_count, axis=0)
    outgoing = (
        jnp.zeros((experts_all * capacity, feature_cols), jnp.bfloat16).at[slot_index].set(picked)
    )
    arrived = move_rows(outgoing.reshape(groups, local_experts, capacity, feature_cols))
    gate_part = jnp.einsum(
        "sxcf,xfh->sxch", arrived, expert_gate, preferred_element_type=jnp.float32
    )
    up_part = jnp.einsum("sxcf,xfh->sxch", arrived, expert_up, preferred_element_type=jnp.float32)
    gate_pre, up_pre = (
        lax.psum(gate_part.astype(jnp.bfloat16), "tok").astype(jnp.float32),
        lax.psum(up_part.astype(jnp.bfloat16), "tok").astype(jnp.float32),
    )
    hidden = (jax.nn.silu(gate_pre) * up_pre).astype(jnp.bfloat16)
    results = jnp.einsum(
        "sxch,xhf->sxcf", hidden, expert_down, preferred_element_type=jnp.float32
    ).astype(jnp.bfloat16)
    returned = move_rows(results).reshape(experts_all * capacity, feature_cols)
    fetched = returned[slot_index].astype(jnp.float32).reshape(row_count, top_count, feature_cols)
    combined = jnp.sum(fetched * gate_values[:, :, None], axis=1)
    return combined.astype(jnp.bfloat16)


VMEM = pl.BlockSpec(memory_space=pltpu.VMEM)
LEFT = pl.BlockSpec(memory_space=pltpu.HBM)
LANES = 128


def call(kernel, out_shape, *operands, scratch=(), left=()):
    operands = [
        pltpu.with_memory_space_constraint(a, pltpu.HBM) if i in left else a
        for i, a in enumerate(operands)
    ]
    return pl.pallas_call(
        kernel,
        out_shape=out_shape,
        in_specs=[LEFT if i in left else VMEM for i in range(len(operands))],
        out_specs=jax.tree.map(lambda _: VMEM, out_shape),
        scratch_shapes=scratch,
        compiler_params=pltpu.CompilerParams(vmem_limit_bytes=16 * 1024 * 1024),
        cost_estimate=pl.CostEstimate(flops=1, bytes_accessed=1, transcendentals=0),
    )(*operands)


class Chain:
    def __init__(self):
        self.token = None

    def call(self, kernel, out_shape, *operands, scratch=(), left=(), last=False):
        count = len(operands)
        ahead = () if self.token is None else (self.token,)

        def ended(*refs):
            kernel(*refs[:count], *refs[count + len(ahead) :])

        if last:
            return call(ended, out_shape, *operands, *ahead, scratch=scratch, left=left)

        def chained(*refs):
            token_ref, outs = refs[count + len(ahead)], refs[count + len(ahead) + 1 :]
            token_ref[...] = jnp.zeros_like(token_ref)
            kernel(*refs[:count], *outs)

        token = jax.ShapeDtypeStruct((8, LANES), jnp.float32)
        self.token, *results = call(
            chained, [token, *out_shape], *operands, *ahead, scratch=scratch, left=left
        )
        return results


def dot(rows, weights):
    return jnp.dot(rows, weights, preferred_element_type=jnp.float32)


def share(core, rows):
    return pl.ds(pl.multiple_of(core * rows, rows), rows)


def pack_kernel(
    own_ref, other_ref, ids_ref, gates_ref, out_ref, ids_mine, gates_mine, table_ref, sems, *,
    experts_all
):
    rows, cols = out_ref.shape[0], own_ref.shape[1]
    mine = share(lax.axis_index("tok") % CORES, rows)
    copies = [
        pltpu.make_async_copy(source, target, sems.at[i])
        for i, (source, target) in enumerate(
            (
                (ids_ref, ids_mine),
                (gates_ref, gates_mine),
                (own_ref.at[mine, :], out_ref.at[:, pl.ds(0, cols)]),
            )
        )
    ]
    for copy in copies:
        copy.start()
    out_ref[:, cols : 2 * cols] = other_ref[mine, :]
    copies[0].wait()
    copies[1].wait()
    line = lax.broadcasted_iota(jnp.int32, (2 * experts_all, table_ref.shape[0]), 0)
    expert = lax.rem(line, experts_all)
    weight = jnp.zeros(line.shape, jnp.float32)
    for k in range(ids_mine.shape[0]):
        weight += jnp.where(ids_mine[k : k + 1, :] == expert, gates_mine[k : k + 1, :], 0.0)
    high = weight.astype(jnp.bfloat16).astype(jnp.float32)
    table_ref[...] = jnp.zeros_like(table_ref)
    table_ref[:, : 2 * experts_all] = jnp.where(line < experts_all, high, weight - high).T
    out_ref[:, 2 * cols :] = table_ref[mine, :].astype(jnp.bfloat16)
    copies[2].wait()


def first_part_kernel(
    message_ref, gate_ref, other_gate_ref, up_ref, other_up_ref, out_ref, gate_out, up_out, sems
):
    cols = gate_ref.shape[1]
    copies = [
        pltpu.make_async_copy(source.at[x], target.at[x], sems.at[i, x])
        for i, (source, target) in enumerate(((gate_ref, gate_out), (up_ref, up_out)))
        for x in range(gate_ref.shape[0])
    ]
    for copy in copies:
        copy.start()
    own, other = message_ref[:, :cols], message_ref[:, cols : 2 * cols]
    places = [(i, x) for i in range(2) for x in range(gate_ref.shape[0])]
    products = [dot(other, (other_gate_ref, other_up_ref)[i][x]) for i, x in places]
    for (i, x), copy, product in zip(places, copies, products, strict=True):
        copy.wait()
        product += dot(own, (gate_out, up_out)[i][x])
        out_ref[i, x] = product.astype(out_ref.dtype)


def part_kernel(message_ref, gate_ref, other_gate_ref, up_ref, other_up_ref, out_ref):
    cols = gate_ref.shape[1]
    own, other = message_ref[:, :cols], message_ref[:, cols : 2 * cols]
    for i, (own_ref, other_ref) in enumerate(
        ((gate_ref, other_gate_ref), (up_ref, other_up_ref))
    ):
        for x in range(gate_ref.shape[0]):
            product = dot(own, own_ref[x]) + dot(other, other_ref[x])
            out_ref[i, x] = product.astype(out_ref.dtype)


def down_kernel(message_ref, down_ref, other_down_ref, *refs, count, experts_all):
    parts = refs[:count]
    *_, out_ref = outs = refs[count:]
    local_experts, _, cols = down_ref.shape
    first = lax.axis_index("exp") * local_experts
    table = message_ref[:, 2 * cols :].astype(jnp.float32)
    lane = lax.broadcasted_iota(jnp.int32, table.shape, 1)
    own, other = 0.0, 0.0
    for x in range(local_experts):
        chosen = (lane == first + x) | (lane == first + x + experts_all)
        weight = jnp.sum(jnp.where(chosen, table, 0.0), axis=1, keepdims=True)
        gate = sum(part[0, x].astype(jnp.float32) for part in parts)
        up = sum(part[1, x].astype(jnp.float32) for part in parts)
        hidden = (gate / (1.0 + jnp.exp(-gate)) * up * weight).astype(jnp.bfloat16)
        own += dot(hidden, down_ref[x])
        other += dot(hidden, other_down_ref[x])
    own_ref, other_ref = outs if len(outs) > 1 else (out_ref.at[:, :cols], out_ref.at[:, cols:])
    own_ref[...] = own.astype(out_ref.dtype)
    other_ref[...] = other.astype(out_ref.dtype)


def total_kernel(*refs):
    results, (keep_ref, send_ref) = refs[:-2], refs[-2:]
    cols = keep_ref.shape[1]
    for out_ref, part in ((keep_ref, slice(0, cols)), (send_ref, slice(cols, None))):
        total = sum(result[:, part].astype(jnp.float32) for result in results)
        out_ref[...] = total.astype(out_ref.dtype)


def place_kernel(keep_ref, taken_ref, last_keep_ref, last_taken_ref, out_ref):
    core, rows = lax.axis_index("tok") % CORES, keep_ref.shape[0]
    kept = keep_ref[...] + last_keep_ref[...].astype(jnp.float32)
    taken = taken_ref[...] + last_taken_ref[...].astype(jnp.float32)
    out_ref[share(core, rows), :] = kept.astype(out_ref.dtype)
    out_ref[share(1 - core, rows), :] = taken.astype(out_ref.dtype)


def exchange(array, axes, distance):
    if isinstance(axes, str):
        axes, distance = (axes,), (distance,)
    indices = np.arange(math.prod(map(lax.axis_size, axes))).reshape([*map(lax.axis_size, axes)])
    others = indices[np.ix_(*(np.arange(n) ^ d for n, d in zip(indices.shape, distance)))]
    pairs = zip(indices.ravel().tolist(), others.ravel().tolist(), strict=True)
    return lax.ppermute(array, axes, list(pairs))


def after(array, *ready):
    return lax.optimization_barrier((array, *ready))[0] if ready else array


def dense_plan(activations, expert_ids, gate_values, expert_gate, expert_up, expert_down):
    row_count, feature_cols = activations.shape
    local_experts, _, hidden_cols = expert_gate.shape
    groups = lax.axis_size("exp")
    chips = lax.axis_size("tok") // CORES
    experts_all = local_experts * groups
    rows = row_count // CORES
    table_cols = -(-2 * experts_all // LANES) * LANES

    other_rows = exchange(activations, "tok", 1)
    chain = Chain()
    (message,) = chain.call(
        functools.partial(pack_kernel, experts_all=experts_all),
        [jax.ShapeDtypeStruct((rows, 2 * feature_cols + table_cols), jnp.bfloat16)],
        activations,
        other_rows,
        expert_ids.T,
        gate_values.T,
        scratch=[
            pltpu.VMEM(expert_ids.shape[::-1], jnp.int32),
            pltpu.VMEM(gate_values.shape[::-1], jnp.float32),
            pltpu.VMEM((row_count, table_cols), jnp.float32),
            pltpu.SemaphoreType.DMA((3,)),
        ],
        left=(0, 2, 3),
    )
    gate, up, down = (
        [own, exchange(after(own, other_rows), "tok", 1)]
        for own in (expert_gate, expert_up, expert_down)
    )
    far = groups // 2
    messages = {0: message}

    def relay(distance, steps, *ready):
        while distance:
            for step in list(steps):
                moved = exchange(after(messages[step], *ready), "exp", distance)
                messages[step ^ distance] = moved
                steps.append(step ^ distance)
            distance //= 2

    if far:
        messages[far] = exchange(message, "exp", far)
        relay(far // 2, [far])
    parts, results = {}, {}

    def multiply(step):
        part = jax.ShapeDtypeStruct((2, local_experts, rows, hidden_cols), jnp.bfloat16)
        if parts:
            (part,) = chain.call(part_kernel, [part], messages[step], *gate, *up)
        else:
            own = [jax.ShapeDtypeStruct(w.shape, w.dtype) for w in (expert_gate, expert_up)]
            part, gate[0], up[0] = chain.call(
                first_part_kernel,
                [part, *own],
                messages[step],
                *gate,
                *up,
                scratch=[pltpu.SemaphoreType.DMA((2, local_experts))],
                left=(1, 3),
            )
        others = [exchange(part, "tok", chip * CORES) for chip in range(1, chips)]
        parts[step] = [part, *others]

    def finish(step):
        dtype = jnp.bfloat16 if step else jnp.float32
        pieces = 2 if step == order[-1] else 1
        shape = jax.ShapeDtypeStruct((rows, 2 * feature_cols // pieces), dtype)
        result = chain.call(
            functools.partial(
                down_kernel, count=len(parts[step]), experts_all=experts_all
            ),
            [shape] * pieces,
            messages[step],
            *down,
            *parts[step],
            last=pieces == 2,
        )
        if pieces == 2:
            results[step] = (
                exchange(result[0], "exp", step),
                exchange(result[1], ("exp", "tok"), (step, 1)),
            )
        else:
            results[step] = exchange(result[0], "exp", step) if step else result[0]

    order = list(dict.fromkeys([0, far, *range(2, groups), min(1, far)]))
    ahead = 2
    for step in order[:ahead]:
        multiply(step)
    relay(far // 2, [0], *(parts[step][0] for step in order[1:ahead]))
    for i, step in enumerate(order):
        finish(step)
        for later in order[ahead + i : ahead + i + 1]:
            multiply(later)
    last_keep, last_taken = results.pop(order[-1])
    keep, send = call(
        total_kernel,
        [
            jax.ShapeDtypeStruct((rows, feature_cols), jnp.float32),
            jax.ShapeDtypeStruct((rows, feature_cols), jnp.bfloat16),
        ],
        *results.values(),
    )
    return call(
        place_kernel,
        jax.ShapeDtypeStruct((row_count, feature_cols), jnp.bfloat16),
        keep,
        exchange(send, "tok", 1),
        last_keep,
        last_taken,
    )


def shards(activations, expert_ids, gate_values, expert_gate, expert_up, expert_down):
    row_count = activations.shape[0]
    local_experts = expert_gate.shape[0]
    groups, pieces = lax.axis_size("exp"), lax.axis_size("tok")
    capacity = 2 * row_count * expert_ids.shape[1] // (local_experts * groups)
    arrays = (activations, expert_ids, gate_values, expert_gate, expert_up, expert_down)
    paired = groups > 1 and groups & (groups - 1) == 0 and pieces & (pieces - 1) == 0 and pieces >= CORES
    if capacity >= row_count and row_count % (16 * CORES) == 0 and paired:
        return dense_plan(*arrays)
    return slot_plan(*arrays, capacity)


def solution(mesh):
    placed = (
        P(("group", "exp"), "tok"),
        P(("group", "exp"), None),
        P(("group", "exp"), None),
        P("exp", "tok", None),
        P("exp", "tok", None),
        P("exp", None, "tok"),
    )
    return jax.shard_map(
        shards, mesh=mesh, in_specs=placed, out_specs=P(("group", "exp"), "tok"), check_vma=False
    )
```

```python
import functools
import math

import jax
import jax.numpy as jnp
import numpy as np
from jax import lax
from jax.experimental import pallas as pl
from jax.experimental.pallas import tpu as pltpu
from jax.sharding import PartitionSpec as P

CORES = 2


def slot_positions(expert_ids, experts_all, capacity):
    flat_ids = expert_ids.reshape(-1)
    one_hot = (flat_ids[:, None] == jnp.arange(experts_all, dtype=jnp.int32)[None, :]).astype(
        jnp.int32
    )
    earlier = jnp.cumsum(one_hot, axis=0) - one_hot
    rank_within = jnp.sum(earlier * one_hot, axis=1)
    return flat_ids * capacity + rank_within


def move_rows(buffer):
    return lax.all_to_all(buffer, "exp", split_axis=0, concat_axis=0, tiled=True)


def slot_plan(activations, expert_ids, gate_values, expert_gate, expert_up, expert_down, capacity):
    row_count, feature_cols = activations.shape
    top_count = expert_ids.shape[1]
    local_experts = expert_gate.shape[0]
    groups = lax.axis_size("exp")
    experts_all = local_experts * groups
    slot_index = slot_positions(expert_ids, experts_all, capacity)
    picked = jnp.repeat(activations, top_count, axis=0)
    outgoing = (
        jnp.zeros((experts_all * capacity, feature_cols), jnp.bfloat16).at[slot_index].set(picked)
    )
    arrived = move_rows(outgoing.reshape(groups, local_experts, capacity, feature_cols))
    gate_part = jnp.einsum(
        "sxcf,xfh->sxch", arrived, expert_gate, preferred_element_type=jnp.float32
    )
    up_part = jnp.einsum("sxcf,xfh->sxch", arrived, expert_up, preferred_element_type=jnp.float32)
    gate_pre, up_pre = (
        lax.psum(gate_part.astype(jnp.bfloat16), "tok").astype(jnp.float32),
        lax.psum(up_part.astype(jnp.bfloat16), "tok").astype(jnp.float32),
    )
    hidden = (jax.nn.silu(gate_pre) * up_pre).astype(jnp.bfloat16)
    results = jnp.einsum(
        "sxch,xhf->sxcf", hidden, expert_down, preferred_element_type=jnp.float32
    ).astype(jnp.bfloat16)
    returned = move_rows(results).reshape(experts_all * capacity, feature_cols)
    fetched = returned[slot_index].astype(jnp.float32).reshape(row_count, top_count, feature_cols)
    combined = jnp.sum(fetched * gate_values[:, :, None], axis=1)
    return combined.astype(jnp.bfloat16)


VMEM = pl.BlockSpec(memory_space=pltpu.VMEM)
LEFT = pl.BlockSpec(memory_space=pltpu.HBM)
LANES = 128


def call(kernel, out_shape, *operands, scratch=(), left=()):
    operands = [
        pltpu.with_memory_space_constraint(a, pltpu.HBM) if i in left else a
        for i, a in enumerate(operands)
    ]
    return pl.pallas_call(
        kernel,
        out_shape=out_shape,
        in_specs=[LEFT if i in left else VMEM for i in range(len(operands))],
        out_specs=jax.tree.map(lambda _: VMEM, out_shape),
        scratch_shapes=scratch,
        compiler_params=pltpu.CompilerParams(vmem_limit_bytes=16 * 1024 * 1024),
        cost_estimate=pl.CostEstimate(flops=1, bytes_accessed=1, transcendentals=0),
    )(*operands)


class Chain:
    def __init__(self):
        self.token = None

    def call(self, kernel, out_shape, *operands, scratch=(), left=(), last=False):
        count = len(operands)
        ahead = () if self.token is None else (self.token,)

        def ended(*refs):
            kernel(*refs[:count], *refs[count + len(ahead) :])

        if last:
            return call(ended, out_shape, *operands, *ahead, scratch=scratch, left=left)

        def chained(*refs):
            token_ref, outs = refs[count + len(ahead)], refs[count + len(ahead) + 1 :]
            token_ref[...] = jnp.zeros_like(token_ref)
            kernel(*refs[:count], *outs)

        token = jax.ShapeDtypeStruct((8, LANES), jnp.float32)
        self.token, *results = call(
            chained, [token, *out_shape], *operands, *ahead, scratch=scratch, left=left
        )
        return results


def dot(rows, weights):
    return jnp.dot(rows, weights, preferred_element_type=jnp.float32)


def share(core, rows):
    return pl.ds(pl.multiple_of(core * rows, rows), rows)


def pack_kernel(
    own_ref, other_ref, ids_ref, gates_ref, out_ref, ids_mine, gates_mine, table_ref, sems, *,
    experts_all
):
    rows, cols = out_ref.shape[0], own_ref.shape[1]
    mine = share(lax.axis_index("tok") % CORES, rows)
    copies = [
        pltpu.make_async_copy(source, target, sems.at[i])
        for i, (source, target) in enumerate(
            (
                (ids_ref, ids_mine),
                (gates_ref, gates_mine),
                (own_ref.at[mine, :], out_ref.at[:, pl.ds(0, cols)]),
            )
        )
    ]
    for copy in copies:
        copy.start()
    out_ref[:, cols : 2 * cols] = other_ref[mine, :]
    copies[0].wait()
    copies[1].wait()
    line = lax.broadcasted_iota(jnp.int32, (2 * experts_all, table_ref.shape[0]), 0)
    expert = lax.rem(line, experts_all)
    weight = jnp.zeros(line.shape, jnp.float32)
    for k in range(ids_mine.shape[0]):
        weight += jnp.where(ids_mine[k : k + 1, :] == expert, gates_mine[k : k + 1, :], 0.0)
    high = weight.astype(jnp.bfloat16).astype(jnp.float32)
    table_ref[...] = jnp.zeros_like(table_ref)
    table_ref[:, : 2 * experts_all] = jnp.where(line < experts_all, high, weight - high).T
    out_ref[:, 2 * cols :] = table_ref[mine, :].astype(jnp.bfloat16)
    copies[2].wait()


def first_part_kernel(
    message_ref, gate_ref, other_gate_ref, up_ref, other_up_ref, out_ref, gate_out, up_out, sems
):
    cols = gate_ref.shape[1]
    copies = [
        pltpu.make_async_copy(source.at[x], target.at[x], sems.at[i, x])
        for i, (source, target) in enumerate(((gate_ref, gate_out), (up_ref, up_out)))
        for x in range(gate_ref.shape[0])
    ]
    for copy in copies:
        copy.start()
    own, other = message_ref[:, :cols], message_ref[:, cols : 2 * cols]
    places = [(i, x) for i in range(2) for x in range(gate_ref.shape[0])]
    products = [dot(other, (other_gate_ref, other_up_ref)[i][x]) for i, x in places]
    for (i, x), copy, product in zip(places, copies, products, strict=True):
        copy.wait()
        product += dot(own, (gate_out, up_out)[i][x])
        out_ref[i, x] = product.astype(out_ref.dtype)


def part_kernel(message_ref, gate_ref, other_gate_ref, up_ref, other_up_ref, out_ref):
    cols = gate_ref.shape[1]
    own, other = message_ref[:, :cols], message_ref[:, cols : 2 * cols]
    for i, (own_ref, other_ref) in enumerate(
        ((gate_ref, other_gate_ref), (up_ref, other_up_ref))
    ):
        for x in range(gate_ref.shape[0]):
            product = dot(own, own_ref[x]) + dot(other, other_ref[x])
            out_ref[i, x] = product.astype(out_ref.dtype)


def down_kernel(message_ref, down_ref, other_down_ref, *refs, count, experts_all):
    parts = refs[:count]
    *_, out_ref = outs = refs[count:]
    local_experts, _, cols = down_ref.shape
    first = lax.axis_index("exp") * local_experts
    table = message_ref[:, 2 * cols :].astype(jnp.float32)
    lane = lax.broadcasted_iota(jnp.int32, table.shape, 1)
    own, other = 0.0, 0.0
    for x in range(local_experts):
        chosen = (lane == first + x) | (lane == first + x + experts_all)
        weight = jnp.sum(jnp.where(chosen, table, 0.0), axis=1, keepdims=True)
        gate = sum(part[0, x].astype(jnp.float32) for part in parts)
        up = sum(part[1, x].astype(jnp.float32) for part in parts)
        hidden = (gate / (1.0 + jnp.exp(-gate)) * up * weight).astype(jnp.bfloat16)
        own += dot(hidden, down_ref[x])
        other += dot(hidden, other_down_ref[x])
    own_ref, other_ref = outs if len(outs) > 1 else (out_ref.at[:, :cols], out_ref.at[:, cols:])
    own_ref[...] = own.astype(out_ref.dtype)
    other_ref[...] = other.astype(out_ref.dtype)


def total_kernel(*refs):
    results, (keep_ref, send_ref) = refs[:-2], refs[-2:]
    cols = keep_ref.shape[1]
    for out_ref, part in ((keep_ref, slice(0, cols)), (send_ref, slice(cols, None))):
        total = sum(result[:, part].astype(jnp.float32) for result in results)
        out_ref[...] = total.astype(out_ref.dtype)


def place_kernel(keep_ref, taken_ref, last_keep_ref, last_taken_ref, out_ref):
    core, rows = lax.axis_index("tok") % CORES, keep_ref.shape[0]
    kept = keep_ref[...] + last_keep_ref[...].astype(jnp.float32)
    taken = taken_ref[...] + last_taken_ref[...].astype(jnp.float32)
    out_ref[share(core, rows), :] = kept.astype(out_ref.dtype)
    out_ref[share(1 - core, rows), :] = taken.astype(out_ref.dtype)


def exchange(array, axes, distance):
    if isinstance(axes, str):
        axes, distance = (axes,), (distance,)
    indices = np.arange(math.prod(map(lax.axis_size, axes))).reshape([*map(lax.axis_size, axes)])
    others = indices[np.ix_(*(np.arange(n) ^ d for n, d in zip(indices.shape, distance)))]
    pairs = zip(indices.ravel().tolist(), others.ravel().tolist(), strict=True)
    return lax.ppermute(array, axes, list(pairs))


def after(array, *ready):
    return lax.optimization_barrier((array, *ready))[0] if ready else array


def dense_plan(activations, expert_ids, gate_values, expert_gate, expert_up, expert_down):
    row_count, feature_cols = activations.shape
    local_experts, _, hidden_cols = expert_gate.shape
    groups = lax.axis_size("exp")
    chips = lax.axis_size("tok") // CORES
    experts_all = local_experts * groups
    rows = row_count // CORES
    table_cols = -(-2 * experts_all // LANES) * LANES

    other_rows = exchange(activations, "tok", 1)
    chain = Chain()
    (message,) = chain.call(
        functools.partial(pack_kernel, experts_all=experts_all),
        [jax.ShapeDtypeStruct((rows, 2 * feature_cols + table_cols), jnp.bfloat16)],
        activations,
        other_rows,
        expert_ids.T,
        gate_values.T,
        scratch=[
            pltpu.VMEM(expert_ids.shape[::-1], jnp.int32),
            pltpu.VMEM(gate_values.shape[::-1], jnp.float32),
            pltpu.VMEM((row_count, table_cols), jnp.float32),
            pltpu.SemaphoreType.DMA((3,)),
        ],
        left=(0, 2, 3),
    )
    gate, up, down = (
        [own, exchange(after(own, other_rows), "tok", 1)]
        for own in (expert_gate, expert_up, expert_down)
    )
    far = groups // 2
    messages = {0: message}

    def relay(distance, steps, *ready):
        while distance:
            for step in list(steps):
                moved = exchange(after(messages[step], *ready), "exp", distance)
                messages[step ^ distance] = moved
                steps.append(step ^ distance)
            distance //= 2

    if far:
        messages[far] = exchange(message, "exp", far)
        relay(far // 2, [far])
    parts, results = {}, {}

    def multiply(step):
        part = jax.ShapeDtypeStruct((2, local_experts, rows, hidden_cols), jnp.bfloat16)
        if parts:
            (part,) = chain.call(part_kernel, [part], messages[step], *gate, *up)
        else:
            own = [jax.ShapeDtypeStruct(w.shape, w.dtype) for w in (expert_gate, expert_up)]
            part, gate[0], up[0] = chain.call(
                first_part_kernel,
                [part, *own],
                messages[step],
                *gate,
                *up,
                scratch=[pltpu.SemaphoreType.DMA((2, local_experts))],
                left=(1, 3),
            )
        others = [exchange(part, "tok", chip * CORES) for chip in range(1, chips)]
        parts[step] = [part, *others]

    def finish(step):
        dtype = jnp.bfloat16 if step else jnp.float32
        pieces = 2 if step == order[-1] else 1
        shape = jax.ShapeDtypeStruct((rows, 2 * feature_cols // pieces), dtype)
        result = chain.call(
            functools.partial(
                down_kernel, count=len(parts[step]), experts_all=experts_all
            ),
            [shape] * pieces,
            messages[step],
            *down,
            *parts[step],
            last=pieces == 2,
        )
        if pieces == 2:
            results[step] = (
                exchange(result[0], "exp", step),
                exchange(result[1], ("exp", "tok"), (step, 1)),
            )
        else:
            results[step] = exchange(result[0], "exp", step) if step else result[0]

    order = list(dict.fromkeys([0, far, *range(2, groups), min(1, far)]))
    ahead = 2
    for step in order[:ahead]:
        multiply(step)
    relay(far // 2, [0], *(moved for step, moved in messages.items() if step))
    for i, step in enumerate(order):
        finish(step)
        for later in order[ahead + i : ahead + i + 1]:
            multiply(later)
    last_keep, last_taken = results.pop(order[-1])
    keep, send = call(
        total_kernel,
        [
            jax.ShapeDtypeStruct((rows, feature_cols), jnp.float32),
            jax.ShapeDtypeStruct((rows, feature_cols), jnp.bfloat16),
        ],
        *results.values(),
    )
    return call(
        place_kernel,
        jax.ShapeDtypeStruct((row_count, feature_cols), jnp.bfloat16),
        keep,
        exchange(send, "tok", 1),
        last_keep,
        last_taken,
    )


def shards(activations, expert_ids, gate_values, expert_gate, expert_up, expert_down):
    row_count = activations.shape[0]
    local_experts = expert_gate.shape[0]
    groups, pieces = lax.axis_size("exp"), lax.axis_size("tok")
    capacity = 2 * row_count * expert_ids.shape[1] // (local_experts * groups)
    arrays = (activations, expert_ids, gate_values, expert_gate, expert_up, expert_down)
    paired = groups > 1 and groups & (groups - 1) == 0 and pieces & (pieces - 1) == 0 and pieces >= CORES
    if capacity >= row_count and row_count % (16 * CORES) == 0 and paired:
        return dense_plan(*arrays)
    return slot_plan(*arrays, capacity)


def solution(mesh):
    placed = (
        P(("group", "exp"), "tok"),
        P(("group", "exp"), None),
        P(("group", "exp"), None),
        P("exp", "tok", None),
        P("exp", "tok", None),
        P("exp", None, "tok"),
    )
    return jax.shard_map(
        shards, mesh=mesh, in_specs=placed, out_specs=P(("group", "exp"), "tok"), check_vma=False
    )
```

```python
import functools
import math

import jax
import jax.numpy as jnp
import numpy as np
from jax import lax
from jax.experimental import pallas as pl
from jax.experimental.pallas import tpu as pltpu
from jax.sharding import PartitionSpec as P

CORES = 2


def slot_positions(expert_ids, experts_all, capacity):
    flat_ids = expert_ids.reshape(-1)
    one_hot = (flat_ids[:, None] == jnp.arange(experts_all, dtype=jnp.int32)[None, :]).astype(
        jnp.int32
    )
    earlier = jnp.cumsum(one_hot, axis=0) - one_hot
    rank_within = jnp.sum(earlier * one_hot, axis=1)
    return flat_ids * capacity + rank_within


def move_rows(buffer):
    return lax.all_to_all(buffer, "exp", split_axis=0, concat_axis=0, tiled=True)


def slot_plan(activations, expert_ids, gate_values, expert_gate, expert_up, expert_down, capacity):
    row_count, feature_cols = activations.shape
    top_count = expert_ids.shape[1]
    local_experts = expert_gate.shape[0]
    groups = lax.axis_size("exp")
    experts_all = local_experts * groups
    slot_index = slot_positions(expert_ids, experts_all, capacity)
    picked = jnp.repeat(activations, top_count, axis=0)
    outgoing = (
        jnp.zeros((experts_all * capacity, feature_cols), jnp.bfloat16).at[slot_index].set(picked)
    )
    arrived = move_rows(outgoing.reshape(groups, local_experts, capacity, feature_cols))
    gate_part = jnp.einsum(
        "sxcf,xfh->sxch", arrived, expert_gate, preferred_element_type=jnp.float32
    )
    up_part = jnp.einsum("sxcf,xfh->sxch", arrived, expert_up, preferred_element_type=jnp.float32)
    gate_pre, up_pre = (
        lax.psum(gate_part.astype(jnp.bfloat16), "tok").astype(jnp.float32),
        lax.psum(up_part.astype(jnp.bfloat16), "tok").astype(jnp.float32),
    )
    hidden = (jax.nn.silu(gate_pre) * up_pre).astype(jnp.bfloat16)
    results = jnp.einsum(
        "sxch,xhf->sxcf", hidden, expert_down, preferred_element_type=jnp.float32
    ).astype(jnp.bfloat16)
    returned = move_rows(results).reshape(experts_all * capacity, feature_cols)
    fetched = returned[slot_index].astype(jnp.float32).reshape(row_count, top_count, feature_cols)
    combined = jnp.sum(fetched * gate_values[:, :, None], axis=1)
    return combined.astype(jnp.bfloat16)


VMEM = pl.BlockSpec(memory_space=pltpu.VMEM)
LEFT = pl.BlockSpec(memory_space=pltpu.HBM)
LANES = 128


def call(kernel, out_shape, *operands, scratch=(), left=()):
    operands = [
        pltpu.with_memory_space_constraint(a, pltpu.HBM) if i in left else a
        for i, a in enumerate(operands)
    ]
    return pl.pallas_call(
        kernel,
        out_shape=out_shape,
        in_specs=[LEFT if i in left else VMEM for i in range(len(operands))],
        out_specs=jax.tree.map(lambda _: VMEM, out_shape),
        scratch_shapes=scratch,
        compiler_params=pltpu.CompilerParams(vmem_limit_bytes=16 * 1024 * 1024),
        cost_estimate=pl.CostEstimate(flops=1, bytes_accessed=1, transcendentals=0),
    )(*operands)


class Chain:
    def __init__(self):
        self.token = None

    def call(self, kernel, out_shape, *operands, scratch=(), left=(), last=False):
        count = len(operands)
        ahead = () if self.token is None else (self.token,)

        def ended(*refs):
            kernel(*refs[:count], *refs[count + len(ahead) :])

        if last:
            return call(ended, out_shape, *operands, *ahead, scratch=scratch, left=left)

        def chained(*refs):
            token_ref, outs = refs[count + len(ahead)], refs[count + len(ahead) + 1 :]
            token_ref[...] = jnp.zeros_like(token_ref)
            kernel(*refs[:count], *outs)

        token = jax.ShapeDtypeStruct((8, LANES), jnp.float32)
        self.token, *results = call(
            chained, [token, *out_shape], *operands, *ahead, scratch=scratch, left=left
        )
        return results


def dot(rows, weights):
    return jnp.dot(rows, weights, preferred_element_type=jnp.float32)


def share(core, rows):
    return pl.ds(pl.multiple_of(core * rows, rows), rows)


def pack_kernel(
    own_ref, other_ref, ids_ref, gates_ref, out_ref, ids_mine, gates_mine, table_ref, sems, *,
    experts_all
):
    rows, cols = out_ref.shape[0], own_ref.shape[1]
    mine = share(lax.axis_index("tok") % CORES, rows)
    copies = [
        pltpu.make_async_copy(source, target, sems.at[i])
        for i, (source, target) in enumerate(
            (
                (ids_ref, ids_mine),
                (gates_ref, gates_mine),
                (own_ref.at[mine, :], out_ref.at[:, pl.ds(0, cols)]),
            )
        )
    ]
    for copy in copies:
        copy.start()
    out_ref[:, cols : 2 * cols] = other_ref[mine, :]
    copies[0].wait()
    copies[1].wait()
    line = lax.broadcasted_iota(jnp.int32, (2 * experts_all, table_ref.shape[0]), 0)
    expert = lax.rem(line, experts_all)
    weight = jnp.zeros(line.shape, jnp.float32)
    for k in range(ids_mine.shape[0]):
        weight += jnp.where(ids_mine[k : k + 1, :] == expert, gates_mine[k : k + 1, :], 0.0)
    high = weight.astype(jnp.bfloat16).astype(jnp.float32)
    table_ref[...] = jnp.zeros_like(table_ref)
    table_ref[:, : 2 * experts_all] = jnp.where(line < experts_all, high, weight - high).T
    out_ref[:, 2 * cols :] = table_ref[mine, :].astype(jnp.bfloat16)
    copies[2].wait()


def first_part_kernel(
    message_ref, gate_ref, other_gate_ref, up_ref, other_up_ref, out_ref, gate_out, up_out, sems
):
    cols = gate_ref.shape[1]
    copies = [
        pltpu.make_async_copy(source.at[x], target.at[x], sems.at[i, x])
        for i, (source, target) in enumerate(((gate_ref, gate_out), (up_ref, up_out)))
        for x in range(gate_ref.shape[0])
    ]
    for copy in copies:
        copy.start()
    own, other = message_ref[:, :cols], message_ref[:, cols : 2 * cols]
    places = [(i, x) for i in range(2) for x in range(gate_ref.shape[0])]
    products = [dot(other, (other_gate_ref, other_up_ref)[i][x]) for i, x in places]
    for (i, x), copy, product in zip(places, copies, products, strict=True):
        copy.wait()
        product += dot(own, (gate_out, up_out)[i][x])
        out_ref[i, x] = product.astype(out_ref.dtype)


def part_kernel(message_ref, gate_ref, other_gate_ref, up_ref, other_up_ref, out_ref):
    cols = gate_ref.shape[1]
    own, other = message_ref[:, :cols], message_ref[:, cols : 2 * cols]
    for i, (own_ref, other_ref) in enumerate(
        ((gate_ref, other_gate_ref), (up_ref, other_up_ref))
    ):
        for x in range(gate_ref.shape[0]):
            product = dot(own, own_ref[x]) + dot(other, other_ref[x])
            out_ref[i, x] = product.astype(out_ref.dtype)


def down_kernel(message_ref, down_ref, other_down_ref, *refs, count, experts_all):
    parts = refs[:count]
    *_, out_ref = outs = refs[count:]
    local_experts, _, cols = down_ref.shape
    first = lax.axis_index("exp") * local_experts
    table = message_ref[:, 2 * cols :].astype(jnp.float32)
    lane = lax.broadcasted_iota(jnp.int32, table.shape, 1)
    own, other = 0.0, 0.0
    for x in range(local_experts):
        chosen = (lane == first + x) | (lane == first + x + experts_all)
        weight = jnp.sum(jnp.where(chosen, table, 0.0), axis=1, keepdims=True)
        gate = sum(part[0, x].astype(jnp.float32) for part in parts)
        up = sum(part[1, x].astype(jnp.float32) for part in parts)
        hidden = (gate / (1.0 + jnp.exp(-gate)) * up * weight).astype(jnp.bfloat16)
        own += dot(hidden, down_ref[x])
        other += dot(hidden, other_down_ref[x])
    own_ref, other_ref = outs if len(outs) > 1 else (out_ref.at[:, :cols], out_ref.at[:, cols:])
    own_ref[...] = own.astype(out_ref.dtype)
    other_ref[...] = other.astype(out_ref.dtype)


def total_kernel(*refs):
    results, (keep_ref, *sends) = refs[: -1 - CORES], refs[-1 - CORES :]
    cols, rows = keep_ref.shape[1], sends[0].shape[0]
    keep_ref[...] = sum(result[:, :cols].astype(jnp.float32) for result in results)
    for i, send_ref in enumerate(sends):
        part = slice(i * rows, (i + 1) * rows)
        total = sum(result[part, cols:].astype(jnp.float32) for result in results)
        send_ref[...] = total.astype(send_ref.dtype)


def place_kernel(keep_ref, last_keep_ref, last_taken_ref, *refs):
    taken_refs, out_ref = refs[:-1], refs[-1]
    core, rows = lax.axis_index("tok") % CORES, keep_ref.shape[0]
    kept = keep_ref[...] + last_keep_ref[...].astype(jnp.float32)
    taken = jnp.concatenate([ref[...] for ref in taken_refs]).astype(jnp.float32)
    taken += last_taken_ref[...].astype(jnp.float32)
    out_ref[share(core, rows), :] = kept.astype(out_ref.dtype)
    out_ref[share(1 - core, rows), :] = taken.astype(out_ref.dtype)


def exchange(array, axes, distance):
    if isinstance(axes, str):
        axes, distance = (axes,), (distance,)
    indices = np.arange(math.prod(map(lax.axis_size, axes))).reshape([*map(lax.axis_size, axes)])
    others = indices[np.ix_(*(np.arange(n) ^ d for n, d in zip(indices.shape, distance)))]
    pairs = zip(indices.ravel().tolist(), others.ravel().tolist(), strict=True)
    return lax.ppermute(array, axes, list(pairs))


def after(array, *ready):
    return lax.optimization_barrier((array, *ready))[0] if ready else array


def dense_plan(activations, expert_ids, gate_values, expert_gate, expert_up, expert_down):
    row_count, feature_cols = activations.shape
    local_experts, _, hidden_cols = expert_gate.shape
    groups = lax.axis_size("exp")
    chips = lax.axis_size("tok") // CORES
    experts_all = local_experts * groups
    rows = row_count // CORES
    table_cols = -(-2 * experts_all // LANES) * LANES

    other_rows = exchange(activations, "tok", 1)
    chain = Chain()
    (message,) = chain.call(
        functools.partial(pack_kernel, experts_all=experts_all),
        [jax.ShapeDtypeStruct((rows, 2 * feature_cols + table_cols), jnp.bfloat16)],
        activations,
        other_rows,
        expert_ids.T,
        gate_values.T,
        scratch=[
            pltpu.VMEM(expert_ids.shape[::-1], jnp.int32),
            pltpu.VMEM(gate_values.shape[::-1], jnp.float32),
            pltpu.VMEM((row_count, table_cols), jnp.float32),
            pltpu.SemaphoreType.DMA((3,)),
        ],
        left=(0, 2, 3),
    )
    gate, up, down = (
        [own, exchange(after(own, other_rows), "tok", 1)]
        for own in (expert_gate, expert_up, expert_down)
    )
    far = groups // 2
    messages = {0: message}

    def relay(distance, steps, *ready):
        while distance:
            for step in list(steps):
                moved = exchange(after(messages[step], *ready), "exp", distance)
                messages[step ^ distance] = moved
                steps.append(step ^ distance)
            distance //= 2

    if far:
        messages[far] = exchange(message, "exp", far)
        relay(far // 2, [far])
    parts, results = {}, {}

    def multiply(step):
        part = jax.ShapeDtypeStruct((2, local_experts, rows, hidden_cols), jnp.bfloat16)
        if parts:
            (part,) = chain.call(part_kernel, [part], messages[step], *gate, *up)
        else:
            own = [jax.ShapeDtypeStruct(w.shape, w.dtype) for w in (expert_gate, expert_up)]
            part, gate[0], up[0] = chain.call(
                first_part_kernel,
                [part, *own],
                messages[step],
                *gate,
                *up,
                scratch=[pltpu.SemaphoreType.DMA((2, local_experts))],
                left=(1, 3),
            )
        others = [exchange(part, "tok", chip * CORES) for chip in range(1, chips)]
        parts[step] = [part, *others]

    def finish(step):
        dtype = jnp.bfloat16 if step else jnp.float32
        pieces = 2 if step == order[-1] else 1
        shape = jax.ShapeDtypeStruct((rows, 2 * feature_cols // pieces), dtype)
        result = chain.call(
            functools.partial(
                down_kernel, count=len(parts[step]), experts_all=experts_all
            ),
            [shape] * pieces,
            messages[step],
            *down,
            *parts[step],
            last=pieces == 2,
        )
        if pieces == 2:
            results[step] = (
                exchange(result[0], "exp", step),
                exchange(result[1], ("exp", "tok"), (step, 1)),
            )
        else:
            results[step] = exchange(result[0], "exp", step) if step else result[0]

    order = list(dict.fromkeys([0, far, *range(2, groups), min(1, far)]))
    ahead = 2
    for step in order[:ahead]:
        multiply(step)
    finish(order[0])
    moved = [block for step, block in messages.items() if step]
    relay(far // 2, [0], *moved, results[order[0]])
    for i, step in enumerate(order):
        if i:
            finish(step)
        for later in order[ahead + i : ahead + i + 1]:
            multiply(later)
    last_keep, last_taken = results.pop(order[-1])
    keep, *sends = call(
        total_kernel,
        [
            jax.ShapeDtypeStruct((rows, feature_cols), jnp.float32),
            *[jax.ShapeDtypeStruct((rows // CORES, feature_cols), jnp.bfloat16)] * CORES,
        ],
        *results.values(),
    )
    return call(
        place_kernel,
        jax.ShapeDtypeStruct((row_count, feature_cols), jnp.bfloat16),
        keep,
        last_keep,
        last_taken,
        *(exchange(send, "tok", 1) for send in sends),
    )


def shards(activations, expert_ids, gate_values, expert_gate, expert_up, expert_down):
    row_count = activations.shape[0]
    local_experts = expert_gate.shape[0]
    groups, pieces = lax.axis_size("exp"), lax.axis_size("tok")
    capacity = 2 * row_count * expert_ids.shape[1] // (local_experts * groups)
    arrays = (activations, expert_ids, gate_values, expert_gate, expert_up, expert_down)
    paired = groups > 1 and groups & (groups - 1) == 0 and pieces & (pieces - 1) == 0 and pieces >= CORES
    if capacity >= row_count and row_count % (16 * CORES) == 0 and paired:
        return dense_plan(*arrays)
    return slot_plan(*arrays, capacity)


def solution(mesh):
    placed = (
        P(("group", "exp"), "tok"),
        P(("group", "exp"), None),
        P(("group", "exp"), None),
        P("exp", "tok", None),
        P("exp", "tok", None),
        P("exp", None, "tok"),
    )
    return jax.shard_map(
        shards, mesh=mesh, in_specs=placed, out_specs=P(("group", "exp"), "tok"), check_vma=False
    )
```

```python
import functools
import math

import jax
import jax.numpy as jnp
import numpy as np
from jax import lax
from jax.experimental import pallas as pl
from jax.experimental.pallas import tpu as pltpu
from jax.sharding import PartitionSpec as P

CORES = 2


def slot_positions(expert_ids, experts_all, capacity):
    flat_ids = expert_ids.reshape(-1)
    one_hot = (flat_ids[:, None] == jnp.arange(experts_all, dtype=jnp.int32)[None, :]).astype(
        jnp.int32
    )
    earlier = jnp.cumsum(one_hot, axis=0) - one_hot
    rank_within = jnp.sum(earlier * one_hot, axis=1)
    return flat_ids * capacity + rank_within


def move_rows(buffer):
    return lax.all_to_all(buffer, "exp", split_axis=0, concat_axis=0, tiled=True)


def slot_plan(activations, expert_ids, gate_values, expert_gate, expert_up, expert_down, capacity):
    row_count, feature_cols = activations.shape
    top_count = expert_ids.shape[1]
    local_experts = expert_gate.shape[0]
    groups = lax.axis_size("exp")
    experts_all = local_experts * groups
    slot_index = slot_positions(expert_ids, experts_all, capacity)
    picked = jnp.repeat(activations, top_count, axis=0)
    outgoing = (
        jnp.zeros((experts_all * capacity, feature_cols), jnp.bfloat16).at[slot_index].set(picked)
    )
    arrived = move_rows(outgoing.reshape(groups, local_experts, capacity, feature_cols))
    gate_part = jnp.einsum(
        "sxcf,xfh->sxch", arrived, expert_gate, preferred_element_type=jnp.float32
    )
    up_part = jnp.einsum("sxcf,xfh->sxch", arrived, expert_up, preferred_element_type=jnp.float32)
    gate_pre, up_pre = (
        lax.psum(gate_part.astype(jnp.bfloat16), "tok").astype(jnp.float32),
        lax.psum(up_part.astype(jnp.bfloat16), "tok").astype(jnp.float32),
    )
    hidden = (jax.nn.silu(gate_pre) * up_pre).astype(jnp.bfloat16)
    results = jnp.einsum(
        "sxch,xhf->sxcf", hidden, expert_down, preferred_element_type=jnp.float32
    ).astype(jnp.bfloat16)
    returned = move_rows(results).reshape(experts_all * capacity, feature_cols)
    fetched = returned[slot_index].astype(jnp.float32).reshape(row_count, top_count, feature_cols)
    combined = jnp.sum(fetched * gate_values[:, :, None], axis=1)
    return combined.astype(jnp.bfloat16)


VMEM = pl.BlockSpec(memory_space=pltpu.VMEM)
LEFT = pl.BlockSpec(memory_space=pltpu.HBM)
LANES = 128


def call(kernel, out_shape, *operands, scratch=(), left=()):
    operands = [
        pltpu.with_memory_space_constraint(a, pltpu.HBM) if i in left else a
        for i, a in enumerate(operands)
    ]
    return pl.pallas_call(
        kernel,
        out_shape=out_shape,
        in_specs=[LEFT if i in left else VMEM for i in range(len(operands))],
        out_specs=jax.tree.map(lambda _: VMEM, out_shape),
        scratch_shapes=scratch,
        compiler_params=pltpu.CompilerParams(vmem_limit_bytes=16 * 1024 * 1024),
        cost_estimate=pl.CostEstimate(flops=1, bytes_accessed=1, transcendentals=0),
    )(*operands)


class Chain:
    def __init__(self):
        self.token = None

    def call(self, kernel, out_shape, *operands, scratch=(), left=(), last=False):
        count = len(operands)
        ahead = () if self.token is None else (self.token,)

        def ended(*refs):
            kernel(*refs[:count], *refs[count + len(ahead) :])

        if last:
            return call(ended, out_shape, *operands, *ahead, scratch=scratch, left=left)

        def chained(*refs):
            token_ref, outs = refs[count + len(ahead)], refs[count + len(ahead) + 1 :]
            token_ref[...] = jnp.zeros_like(token_ref)
            kernel(*refs[:count], *outs)

        token = jax.ShapeDtypeStruct((8, LANES), jnp.float32)
        self.token, *results = call(
            chained, [token, *out_shape], *operands, *ahead, scratch=scratch, left=left
        )
        return results


def dot(rows, weights):
    return jnp.dot(rows, weights, preferred_element_type=jnp.float32)


def share(core, rows):
    return pl.ds(pl.multiple_of(core * rows, rows), rows)


def pack_kernel(
    own_ref, other_ref, ids_ref, gates_ref, out_ref, ids_mine, gates_mine, table_ref, sems, *,
    experts_all
):
    rows, cols = out_ref.shape[0], own_ref.shape[1]
    mine = share(lax.axis_index("tok") % CORES, rows)
    copies = [
        pltpu.make_async_copy(source, target, sems.at[i])
        for i, (source, target) in enumerate(
            (
                (ids_ref, ids_mine),
                (gates_ref, gates_mine),
                (own_ref.at[mine, :], out_ref.at[:, pl.ds(0, cols)]),
            )
        )
    ]
    for copy in copies:
        copy.start()
    out_ref[:, cols : 2 * cols] = other_ref[mine, :]
    copies[0].wait()
    copies[1].wait()
    line = lax.broadcasted_iota(jnp.int32, (2 * experts_all, table_ref.shape[0]), 0)
    expert = lax.rem(line, experts_all)
    weight = jnp.zeros(line.shape, jnp.float32)
    for k in range(ids_mine.shape[0]):
        weight += jnp.where(ids_mine[k : k + 1, :] == expert, gates_mine[k : k + 1, :], 0.0)
    high = weight.astype(jnp.bfloat16).astype(jnp.float32)
    table_ref[...] = jnp.zeros_like(table_ref)
    table_ref[:, : 2 * experts_all] = jnp.where(line < experts_all, high, weight - high).T
    out_ref[:, 2 * cols :] = table_ref[mine, :].astype(jnp.bfloat16)
    copies[2].wait()


def first_part_kernel(
    message_ref, gate_ref, other_gate_ref, up_ref, other_up_ref, out_ref, gate_out, up_out, sems
):
    cols = gate_ref.shape[1]
    copies = [
        pltpu.make_async_copy(source.at[x], target.at[x], sems.at[i, x])
        for i, (source, target) in enumerate(((gate_ref, gate_out), (up_ref, up_out)))
        for x in range(gate_ref.shape[0])
    ]
    for copy in copies:
        copy.start()
    own, other = message_ref[:, :cols], message_ref[:, cols : 2 * cols]
    places = [(i, x) for i in range(2) for x in range(gate_ref.shape[0])]
    products = [dot(other, (other_gate_ref, other_up_ref)[i][x]) for i, x in places]
    for (i, x), copy, product in zip(places, copies, products, strict=True):
        copy.wait()
        product += dot(own, (gate_out, up_out)[i][x])
        out_ref[i, x] = product.astype(out_ref.dtype)


def part_kernel(message_ref, gate_ref, other_gate_ref, up_ref, other_up_ref, out_ref):
    cols = gate_ref.shape[1]
    own, other = message_ref[:, :cols], message_ref[:, cols : 2 * cols]
    for i, (own_ref, other_ref) in enumerate(
        ((gate_ref, other_gate_ref), (up_ref, other_up_ref))
    ):
        for x in range(gate_ref.shape[0]):
            product = dot(own, own_ref[x]) + dot(other, other_ref[x])
            out_ref[i, x] = product.astype(out_ref.dtype)


def down_kernel(message_ref, down_ref, other_down_ref, *refs, count, experts_all):
    parts = refs[:count]
    *_, out_ref = outs = refs[count:]
    local_experts, _, cols = down_ref.shape
    first = lax.axis_index("exp") * local_experts
    table = message_ref[:, 2 * cols :].astype(jnp.float32)
    lane = lax.broadcasted_iota(jnp.int32, table.shape, 1)
    hidden = []
    for x in range(local_experts):
        chosen = (lane == first + x) | (lane == first + x + experts_all)
        weight = jnp.sum(jnp.where(chosen, table, 0.0), axis=1, keepdims=True)
        gate = sum(part[0, x].astype(jnp.float32) for part in parts)
        up = sum(part[1, x].astype(jnp.float32) for part in parts)
        hidden.append((gate / (1.0 + jnp.exp(-gate)) * up * weight).astype(jnp.bfloat16))
    hidden = jnp.concatenate(hidden, axis=1)
    own = dot(hidden, down_ref[...].reshape(-1, cols))
    other = dot(hidden, other_down_ref[...].reshape(-1, cols))
    own_ref, other_ref = outs if len(outs) > 1 else (out_ref.at[:, :cols], out_ref.at[:, cols:])
    own_ref[...] = own.astype(out_ref.dtype)
    other_ref[...] = other.astype(out_ref.dtype)


def total_kernel(*refs):
    results, (keep_ref, send_ref) = refs[:-2], refs[-2:]
    cols = keep_ref.shape[1]
    for out_ref, part in ((keep_ref, slice(0, cols)), (send_ref, slice(cols, None))):
        total = sum(result[:, part].astype(jnp.float32) for result in results)
        out_ref[...] = total.astype(out_ref.dtype)


def place_kernel(keep_ref, taken_ref, last_keep_ref, last_taken_ref, out_ref):
    core, rows = lax.axis_index("tok") % CORES, keep_ref.shape[0]
    kept = keep_ref[...] + last_keep_ref[...].astype(jnp.float32)
    taken = taken_ref[...] + last_taken_ref[...].astype(jnp.float32)
    out_ref[share(core, rows), :] = kept.astype(out_ref.dtype)
    out_ref[share(1 - core, rows), :] = taken.astype(out_ref.dtype)


def exchange(array, axes, distance):
    if isinstance(axes, str):
        axes, distance = (axes,), (distance,)
    indices = np.arange(math.prod(map(lax.axis_size, axes))).reshape([*map(lax.axis_size, axes)])
    others = indices[np.ix_(*(np.arange(n) ^ d for n, d in zip(indices.shape, distance)))]
    pairs = zip(indices.ravel().tolist(), others.ravel().tolist(), strict=True)
    return lax.ppermute(array, axes, list(pairs))


def after(array, *ready):
    return lax.optimization_barrier((array, *ready))[0] if ready else array


def dense_plan(activations, expert_ids, gate_values, expert_gate, expert_up, expert_down):
    row_count, feature_cols = activations.shape
    local_experts, _, hidden_cols = expert_gate.shape
    groups = lax.axis_size("exp")
    chips = lax.axis_size("tok") // CORES
    experts_all = local_experts * groups
    rows = row_count // CORES
    table_cols = -(-2 * experts_all // LANES) * LANES

    other_rows = exchange(activations, "tok", 1)
    chain = Chain()
    (message,) = chain.call(
        functools.partial(pack_kernel, experts_all=experts_all),
        [jax.ShapeDtypeStruct((rows, 2 * feature_cols + table_cols), jnp.bfloat16)],
        activations,
        other_rows,
        expert_ids.T,
        gate_values.T,
        scratch=[
            pltpu.VMEM(expert_ids.shape[::-1], jnp.int32),
            pltpu.VMEM(gate_values.shape[::-1], jnp.float32),
            pltpu.VMEM((row_count, table_cols), jnp.float32),
            pltpu.SemaphoreType.DMA((3,)),
        ],
        left=(0, 2, 3),
    )
    gate, up, down = (
        [own, exchange(after(own, other_rows), "tok", 1)]
        for own in (expert_gate, expert_up, expert_down)
    )
    far = groups // 2
    messages = {0: message}

    def relay(distance, steps, *ready):
        while distance:
            for step in list(steps):
                moved = exchange(after(messages[step], *ready), "exp", distance)
                messages[step ^ distance] = moved
                steps.append(step ^ distance)
            distance //= 2

    if far:
        messages[far] = exchange(message, "exp", far)
        relay(far // 2, [far])
    parts, results = {}, {}

    def multiply(step):
        part = jax.ShapeDtypeStruct((2, local_experts, rows, hidden_cols), jnp.bfloat16)
        if parts:
            (part,) = chain.call(part_kernel, [part], messages[step], *gate, *up)
        else:
            own = [jax.ShapeDtypeStruct(w.shape, w.dtype) for w in (expert_gate, expert_up)]
            part, gate[0], up[0] = chain.call(
                first_part_kernel,
                [part, *own],
                messages[step],
                *gate,
                *up,
                scratch=[pltpu.SemaphoreType.DMA((2, local_experts))],
                left=(1, 3),
            )
        others = [exchange(part, "tok", chip * CORES) for chip in range(1, chips)]
        parts[step] = [part, *others]

    def finish(step):
        dtype = jnp.bfloat16 if step else jnp.float32
        pieces = 2 if step == order[-1] else 1
        shape = jax.ShapeDtypeStruct((rows, 2 * feature_cols // pieces), dtype)
        result = chain.call(
            functools.partial(
                down_kernel, count=len(parts[step]), experts_all=experts_all
            ),
            [shape] * pieces,
            messages[step],
            *down,
            *parts[step],
            last=pieces == 2,
        )
        if pieces == 2:
            results[step] = (
                exchange(result[0], "exp", step),
                exchange(result[1], ("exp", "tok"), (step, 1)),
            )
        else:
            results[step] = exchange(result[0], "exp", step) if step else result[0]

    order = list(dict.fromkeys([0, far, *range(2, groups), min(1, far)]))
    ahead = 2
    for step in order[:ahead]:
        multiply(step)
    relay(far // 2, [0], *(moved for step, moved in messages.items() if step))
    for i, step in enumerate(order):
        finish(step)
        for later in order[ahead + i : ahead + i + 1]:
            multiply(later)
    last_keep, last_taken = results.pop(order[-1])
    keep, send = call(
        total_kernel,
        [
            jax.ShapeDtypeStruct((rows, feature_cols), jnp.float32),
            jax.ShapeDtypeStruct((rows, feature_cols), jnp.bfloat16),
        ],
        *results.values(),
    )
    return call(
        place_kernel,
        jax.ShapeDtypeStruct((row_count, feature_cols), jnp.bfloat16),
        keep,
        exchange(send, "tok", 1),
        last_keep,
        last_taken,
    )


def shards(activations, expert_ids, gate_values, expert_gate, expert_up, expert_down):
    row_count = activations.shape[0]
    local_experts = expert_gate.shape[0]
    groups, pieces = lax.axis_size("exp"), lax.axis_size("tok")
    capacity = 2 * row_count * expert_ids.shape[1] // (local_experts * groups)
    arrays = (activations, expert_ids, gate_values, expert_gate, expert_up, expert_down)
    paired = groups > 1 and groups & (groups - 1) == 0 and pieces & (pieces - 1) == 0 and pieces >= CORES
    if capacity >= row_count and row_count % (16 * CORES) == 0 and paired:
        return dense_plan(*arrays)
    return slot_plan(*arrays, capacity)


def solution(mesh):
    placed = (
        P(("group", "exp"), "tok"),
        P(("group", "exp"), None),
        P(("group", "exp"), None),
        P("exp", "tok", None),
        P("exp", "tok", None),
        P("exp", None, "tok"),
    )
    return jax.shard_map(
        shards, mesh=mesh, in_specs=placed, out_specs=P(("group", "exp"), "tok"), check_vma=False
    )
```
